128 devices in a mesh: row: 16 (over z, x), col: 8 (over y, core).
Axes of the slice: x: 4, y: 4, z: 4, core: 2. Of those that a mesh axis runs over, the one named last changes fastest.
Arguments:
- diag_base: float32 [2, 16, 512, 512], P(None, 'row'), as said below
- items: bfloat16 [16, 8, 16, 512, 128], P('row', 'col'), may hold values from -0.8984375 to 0.8984375
- item_rank: int32 [16, 8, 16], P('row', 'col'), may hold values from 16 to 64
- item_owner: int32 [16, 8, 16], P('row', 'col'), may hold values from 0 to 15, as said below
- item_block: int32 [16, 8, 16, 2], P('row', 'col'), may hold values from 0 to 3, as said below
Outputs:
- diag_factors: float32 [2, 512, 512], replicated
- panels: float32 [2, 16, 512, 1024], P(None, 'row')
- trailing_diagonal: float32 [2, 16, 512, 512], P(None, 'row')
- trailing: float32 [2, 16, 4, 8, 512, 512], P(None, 'row', None, 'col')
The draws below stay inside these ranges and needn't reach their ends.
Inputs may be any that keep to these rules, and one draw needn't show every extreme that they name: `item_owner`: the items of one device name each owner at most 2 times, and one owner exactly 2 times. `item_block`: the target block column jl * 8 + c lies strictly below the target block row il * 16 + owner. `diag_base`: symmetric with a positive diagonal that exceeds the sum of the magnitudes of its row's other entries.
All inputs are finite; a program needn't handle non-finite values.
Results may differ from the reference program's by a relative error of at most 0.0007.
Values may be sent and summed in bfloat16 or wider, within the bound.
No kernel may reach another device: no remote copies, remote signals or barrier semaphores. Data moves between devices by JAX's collectives and lax.ppermute only.
A program may use at most 192 MiB of HBM per device.

```python
import jax
import jax.numpy as jnp
from jax import lax

B = 512
R = 64
BR_DEV = 2
ITEMS_DEV = 16
CAP = 2
NBLK = 32
BC_DEV = 4
N_ROW = 16
N_COL = 8


def owners_blocks(key):
    nrow = NBLK // BR_DEV
    ncol = NBLK // BC_DEV
    keys = [jax.random.fold_in(key, 101 + n) for n in range(8)]
    first = jax.random.randint(keys[0], (nrow, ncol), 0, nrow)
    second = jax.random.randint(keys[1], (nrow, ncol), 0, nrow)
    third = jax.random.randint(keys[2], (nrow, ncol), 0, nrow)
    shift = jax.random.randint(keys[3], (), 0, nrow)
    hot = (jnp.minimum(jnp.minimum(first, second), third) + shift) % nrow
    scores = jax.random.randint(keys[4], (nrow, ncol, nrow - 1), 0, 1 << 20) * (nrow - 1) + jnp.arange(nrow - 1)[None, None, :]
    order = jnp.argsort(scores, axis=-1).astype(jnp.int32)
    others = (hot[..., None] + 1 + order) % nrow
    slot = jnp.arange(ITEMS_DEV)
    later = jnp.maximum(slot - CAP, 0) % (nrow - 1)
    picked = jnp.take_along_axis(others, jnp.broadcast_to(later[None, None, :], (nrow, ncol, ITEMS_DEV)), axis=-1)
    owner = jnp.where(slot[None, None, :] < CAP, hot[..., None], picked).astype(jnp.int32)
    holder = jnp.broadcast_to(jnp.arange(ncol)[None, :, None], (nrow, ncol, ITEMS_DEV))
    local_row = jax.random.randint(keys[5], (nrow, ncol, ITEMS_DEV), 0, BR_DEV)
    local_row = jnp.where((local_row == 0) & (owner <= holder), 1, local_row)
    brow = local_row * nrow + owner
    span = (brow - 1 - holder) // ncol + 1
    local_col = jax.random.randint(keys[6], (nrow, ncol, ITEMS_DEV), 0, 1 << 20) % span
    return (owner, jnp.stack([local_row, local_col], axis=-1).astype(jnp.int32))


def draw_item_owner(key, part):
    owner, blocks = owners_blocks(key)
    return owner


def draw_item_block(key, part):
    owner, blocks = owners_blocks(key)
    return blocks


def draw_items(key, part):
    owner, blocks = owners_blocks(key)
    key = jax.random.fold_in(key, 11)
    nrow = NBLK // BR_DEV
    ncol = NBLK // BC_DEV
    holder = jnp.broadcast_to(jnp.arange(ncol)[None, :, None], owner.shape)
    target_row = blocks[..., 0] * nrow + owner
    target_col = blocks[..., 1] * ncol + holder
    strong = (target_row == 1) & (target_col == 0)
    weaker = (target_col == 0) & jnp.logical_not(strong)
    amplitude = jnp.where(strong, 0.45, jnp.where(weaker, 0.045, 0.15)).astype(jnp.float32)
    shape = (nrow, ncol, ITEMS_DEV, B, 2 * R)
    noise_key = jax.random.fold_in(key, 1)
    noise = jax.random.normal(noise_key, shape, jnp.float32)
    values = jnp.clip(amplitude[..., None, None] * noise, -0.8984375, 0.8984375)
    return values.astype(jnp.bfloat16)


def draw_diag_base(key, part):
    nrow = NBLK // BR_DEV
    first = jax.random.fold_in(key, 7)
    second = jax.random.fold_in(key, 8)
    noise = jax.random.uniform(first, (BR_DEV, nrow, B, B), jnp.float32, -1.0, 1.0) * (0.49 / B)
    sym = noise + jnp.swapaxes(noise, -1, -2)
    values = jax.random.uniform(second, (BR_DEV, nrow, B), jnp.float32, 1.0, 3.0)
    eye = jnp.eye(B, dtype=jnp.float32)
    return sym * (1.0 - eye) + eye * values[..., None]


def with_ends(result, key, least, high):
    shape = result.shape
    place = [jax.random.randint(jax.random.fold_in(key, axis), (), 0, shape[axis]) for axis in range(len(shape))]
    result = result.at[tuple(place)].set(least)
    longest = shape.index(max(shape))
    place[longest] = (place[longest] + 1) % shape[longest]
    return result.at[tuple(place)].set(high)


def setup_inputs(seed: int = 0) -> dict:
    streams_of = jax.random.split(jax.random.key(seed), 6)
    return {
        "diag_base": draw_diag_base(jax.random.fold_in(streams_of[5], 71), 0),
        "items": draw_items(jax.random.fold_in(streams_of[5], 71), 0),
        "item_rank": with_ends(jax.random.randint(streams_of[2], (N_ROW, N_COL, ITEMS_DEV), R // 4, R + 1), jax.random.fold_in(streams_of[2], 1), R // 4, R).astype(jnp.int32),
        "item_owner": draw_item_owner(jax.random.fold_in(streams_of[5], 71), 0),
        "item_block": draw_item_block(jax.random.fold_in(streams_of[5], 71), 0),
    }


def reference(diag_base, items, item_rank, item_owner, item_block):
    nblk = NBLK
    cols = jnp.arange(2 * R) % R
    keep = (cols[None, None, None, :] < item_rank[..., None]).astype(jnp.bfloat16)
    factors = items * keep[..., None, :]
    holder = jnp.broadcast_to(jnp.arange(N_COL, dtype=jnp.int32)[None, :, None], item_owner.shape)
    brow = (item_block[..., 0] * N_ROW + item_owner).reshape(-1).astype(jnp.int32)
    bcol = (item_block[..., 1] * N_COL + holder).reshape(-1).astype(jnp.int32)
    flat = factors.reshape(-1, B, 2 * R)
    front = jnp.zeros((nblk, nblk, B, B), jnp.float32)
    diag = diag_base.reshape(nblk, B, B).astype(jnp.float32)

    def add_item(q, carry):
        front, diag = carry
        xfac = flat[q, :, :R]
        yfac = flat[q, :, R:]
        i = brow[q]
        j = bcol[q]
        cross = jnp.dot(xfac.astype(jnp.float32), yfac.T.astype(jnp.float32), preferred_element_type=jnp.float32)
        left = jnp.dot(xfac.astype(jnp.float32), xfac.T.astype(jnp.float32), preferred_element_type=jnp.float32)
        right = jnp.dot(yfac.astype(jnp.float32), yfac.T.astype(jnp.float32), preferred_element_type=jnp.float32)
        front = front.at[i, j].add(cross)
        diag = diag.at[i].add(left).at[j].add(right)
        return (front, diag)
    front, diag = lax.fori_loop(0, flat.shape[0], add_item, (front, diag))
    lowers = []
    panel_list = []
    index = jnp.arange(nblk)
    for k in range(2):
        lower = jnp.linalg.cholesky(diag[k])
        column = front[:, k]
        solved = lax.linalg.triangular_solve(jnp.broadcast_to(lower, column.shape), column, left_side=False, lower=True, transpose_a=True)
        solved = jnp.where((index > k)[:, None, None], solved, jnp.zeros_like(solved))
        diag = diag - jnp.einsum('ipq,irq->ipr', solved, solved, precision=lax.Precision.HIGHEST)

        def update_row(pair):
            row_blocks, own = pair
            return row_blocks - jnp.einsum('pq,jrq->jpr', own, solved, precision=lax.Precision.HIGHEST)
        front = lax.map(update_row, (front, solved))
        lowers.append(lower)
        panel_list.append(solved)
    diag_factors = jnp.stack(lowers)
    panels = jnp.concatenate(panel_list, axis=-1).reshape(BR_DEV, N_ROW, B, 2 * B)
    trailing_diagonal = jnp.where((index >= 2)[:, None, None], diag, jnp.zeros_like(diag)).reshape(BR_DEV, N_ROW, B, B)
    below = (index[:, None] > index[None, :]) & (index[None, :] >= 2)
    trailing = jnp.where(below[:, :, None, None], front, jnp.zeros_like(front)).reshape(BR_DEV, N_ROW, BC_DEV, N_COL, B, B)
    return (diag_factors, panels, trailing_diagonal, trailing)
```

```python
import functools

import jax
import jax.numpy as jnp
from jax import lax
from jax.experimental import pallas as pl
from jax.experimental.pallas import tpu as pltpu
from jax.sharding import PartitionSpec as P

HI = lax.Precision.HIGHEST
N = 512
NB = 128
RANK = 64
WIDTH = 128
LABEL_ROWS = 16
ROWS = N + LABEL_ROWS
CAP = 2
F32 = jnp.float32
BF16 = jnp.bfloat16
VMEM = pl.BlockSpec(memory_space=pltpu.VMEM)
SMEM = pl.BlockSpec(memory_space=pltpu.SMEM)


def dotT(a,b):
    return lax.dot_general(a,b,(((0,),(0,)),((),())),precision=HI,preferred_element_type=F32)
def dot(a,b):
    return lax.dot_general(a,b,(((1,),(0,)),((),())),precision=HI,preferred_element_type=F32)
def lane(x,k):
    return jnp.broadcast_to(x[:,k:k+1],(8,128))
def sub(x,k):
    return jnp.broadcast_to(x[k:k+1,:],(8,x.shape[1]))
def factor_block(d, eye):
    A=[d[8*q:8*q+8,:] for q in range(16)]
    Z=[eye[8*q:8*q+8,:] for q in range(16)]
    sl=lax.broadcasted_iota(jnp.int32,(8,128),0)
    for g in range(4):
        for p in range(4*g,4*g+4):
            S=[lane(A[p],8*p+k) for k in range(8)]
            T={q:[lane(A[q],8*p+k) for k in range(8)] for q in range(p+1,4*g+4)}
            a,z=A[p],Z[p]
            rows=[]
            for j in range(8):
                r=lax.rsqrt(sub(S[j],j))
                c=S[j]*r
                u=[sub(c,m) if m>j else None for m in range(8)]
                for m in range(j+1,8):
                    S[m]=S[m]-c*u[m]
                arow=sub(a,j)*r; zrow=sub(z,j)*r
                cm=jnp.where(sl>j,c,0.0)
                a=jnp.where(sl==j,arow,a-cm*arow)
                z=jnp.where(sl==j,zrow,z-cm*zrow)
                for q in T:
                    t=T[q][j]*r
                    for m in range(j+1,8):
                        T[q][m]=T[q][m]-t*u[m]
                    A[q]=A[q]-t*arow
                    Z[q]=Z[q]-t*zrow
            A[p],Z[p]=a,z
        if g<3:
            ug=jnp.concatenate(A[4*g:4*g+4],axis=0)
            zg=jnp.concatenate(Z[4*g:4*g+4],axis=0)
            both=jnp.concatenate([ug,zg],axis=1)
            upd=dotT(ug,both)
            for q in range(4*g+4,16):
                A[q]=A[q]-upd[8*q:8*q+8,:128]
                Z[q]=Z[q]-upd[8*q:8*q+8,128:]
    return jnp.concatenate(A,axis=0), jnp.concatenate(Z,axis=0)
def chol_into(work,l_ref,inv_ref):
    r128=lax.broadcasted_iota(jnp.int32,(NB,NB),0); c128=lax.broadcasted_iota(jnp.int32,(NB,NB),1)
    eye=jnp.where(r128==c128,1.0,0.0).astype(F32)
    nb=N//NB
    for b in range(nb):
        r0=b*NB; r1=r0+NB
        u,gi=factor_block(work[r0:r1,r0:r1],eye)
        u=jnp.where(c128>=r128,u,0.0); gi=jnp.where(c128<=r128,gi,0.0)
        l_ref[r0:r1,r0:r1]=u.T
        if b+1<nb: l_ref[r0:r1,r1:]=jnp.zeros((NB,N-r1),F32)
        inv_ref[r0:r1,r0:r1]=gi
        if b+1<nb: inv_ref[r0:r1,r1:]=jnp.zeros((NB,N-r1),F32)
        if b:
            inv_ref[r0:r1,:r0]=dot(gi,work[r0:r1,N:N+r0])
        if b+1<nb:
            ur=dot(gi,work[r0:r1,r1:N])
            l_ref[r1:,r0:r1]=ur.T
            work[r1:,r1:N]-=dotT(ur,ur)
            upd=dotT(ur,inv_ref[r0:r1,:r1])
            work[r1:,N:N+r1]-=upd

def params(mib=48):
    return pltpu.CompilerParams(vmem_limit_bytes=mib << 20)


def first_pivot_kernel(d_ref, l_ref, inv_ref, work):
    work[:, :N] = d_ref[...]
    work[:, N:] = jnp.zeros((N, N), F32)
    chol_into(work, l_ref, inv_ref)


def second_pivot_kernel(t_ref, inv0_ref, p_ref, l_ref, inv_ref, work):
    p = mul_t(t_ref[:N, :], inv0_ref[...])
    p_ref[...] = p
    work[:, :N] = t_ref[N:, :] - mul_t(p, p)
    work[:, N:] = jnp.zeros((N, N), F32)
    chol_into(work, l_ref, inv_ref)


def block_shape():
    return jax.ShapeDtypeStruct((N, N), F32)


def first_pivot(d):
    return pl.pallas_call(
        first_pivot_kernel,
        out_shape=(block_shape(),) * 2,
        in_specs=[VMEM],
        out_specs=(VMEM,) * 2,
        scratch_shapes=[pltpu.VMEM((N, 2 * N), F32)],
        compiler_params=params(),
        cost_estimate=pl.CostEstimate(flops=20_000_000_000, bytes_accessed=3 << 20, transcendentals=0),
        name="first_pivot",
    )(d)


def second_pivot(t, inv0):
    return pl.pallas_call(
        second_pivot_kernel,
        out_shape=(block_shape(),) * 3,
        in_specs=[VMEM] * 2,
        out_specs=(VMEM,) * 3,
        scratch_shapes=[pltpu.VMEM((N, 2 * N), F32)],
        compiler_params=params(),
        cost_estimate=pl.CostEstimate(flops=20_000_000_000, bytes_accessed=6 << 20, transcendentals=0),
        name="second_pivot",
    )(t, inv0)


def mul_t(a, b):
    return lax.dot_general(a, b, (((1,), (1,)), ((), ())), precision=HI, preferred_element_type=F32)


def outer(a, b):
    return lax.dot_general(a, b, (((1,), (1,)), ((), ())), preferred_element_type=F32)


def keep_row(rank):
    lanes = lax.broadcasted_iota(jnp.int32, (1, WIDTH), 1)
    within = jnp.where(lanes >= RANK, lanes - RANK, lanes)
    return jnp.where(within < rank, 1.0, 0.0).astype(F32)


def pack_kernel(owner, block, rank, items, out, count):
    nrow = out.shape[0]

    def clear(o, _):
        count[o] = 0
        return 0

    lax.fori_loop(0, nrow, clear, 0)
    for slot in range(CAP):
        out[:, slot, N:, :] = jnp.zeros((nrow, LABEL_ROWS, WIDTH), BF16)

    def place(s, _):
        o = owner[s]
        slot = jnp.minimum(count[o], CAP - 1)
        count[o] = slot + 1
        keep = keep_row(rank[s])
        out[o, slot, :N, :] = items[s] * keep.astype(BF16)
        code = (block[2 * s] * 4 + block[2 * s + 1] + 1).astype(F32)
        out[o, slot, N:, :] = jnp.full((LABEL_ROWS, WIDTH), code, F32).astype(BF16)
        return 0

    lax.fori_loop(0, items.shape[0], place, 0)


def pack(owner, block, rank, items, nrow):
    return pl.pallas_call(
        pack_kernel,
        out_shape=jax.ShapeDtypeStruct((nrow, CAP, ROWS, WIDTH), BF16),
        in_specs=[SMEM, SMEM, SMEM, VMEM],
        out_specs=VMEM,
        scratch_shapes=[pltpu.SMEM((nrow,), jnp.int32)],
        compiler_params=params(),
        cost_estimate=pl.CostEstimate(flops=0, bytes_accessed=6 << 20, transcendentals=0),
        name="pack",
    )(owner, block, rank, items)


def pivot_terms_kernel(owner, block, rank, place, items, base, zero_out, one_out):
    row, col = place[0], place[1]
    zero_out[...] = jnp.zeros((N, N), F32)
    one_out[...] = jnp.zeros((2 * N, N), F32)

    @pl.when((row == 0) & (col == 0))
    def _():
        zero_out[...] = base[...]

    @pl.when((row == 1) & (col == 0))
    def _():
        one_out[N:, :] = base[...]

    def step(s, _):
        first = block[2 * s + 1] == 0
        keep = keep_row(rank[s]).astype(BF16)

        @pl.when(first & (col == 0))
        def _():
            y = (items[s] * keep)[:, RANK:]
            zero_out[...] += outer(y, y)

        @pl.when(first & (col == 1))
        def _():
            y = (items[s] * keep)[:, RANK:]
            one_out[N:, :] += outer(y, y)

        @pl.when(first & (col == 0) & (owner[s] == 1) & (block[2 * s] == 0))
        def _():
            both = items[s] * keep
            x, y = both[:, :RANK], both[:, RANK:]
            one_out[:N, :] += outer(x, y)
            one_out[N:, :] += outer(x, x)

        return 0

    lax.fori_loop(0, items.shape[0], step, 0)


def pivot_terms(owner, block, rank, place, items, base):
    return pl.pallas_call(
        pivot_terms_kernel,
        out_shape=(block_shape(), jax.ShapeDtypeStruct((2 * N, N), F32)),
        in_specs=[SMEM] * 4 + [VMEM] * 2,
        out_specs=(VMEM,) * 2,
        compiler_params=params(),
        cost_estimate=pl.CostEstimate(flops=1_000_000_000, bytes_accessed=6 << 20, transcendentals=0),
        name="pivot_terms",
    )(owner, block, rank, place, items, base)


def column_terms_kernel(block, rank, items, out):
    out[...] = jnp.zeros(out.shape, F32)
    parts, piece = out.shape[0] // 2, out.shape[2]

    def step(s, _):
        jl = block[2 * s + 1]
        il = jl // 2
        h = jl - 2 * il
        y = (items[s] * keep_row(rank[s]).astype(BF16))[:, RANK:]
        at = (pl.ds(h * parts, parts), il)
        out[at] = out[at] + outer(y, y).reshape(parts, piece, N)
        return 0

    lax.fori_loop(0, items.shape[0], step, 0)


def column_terms(block, rank, items, ncol):
    return pl.pallas_call(
        column_terms_kernel,
        out_shape=jax.ShapeDtypeStruct((2 * ncol, 2, N // ncol, N), F32),
        in_specs=[SMEM] * 2 + [VMEM],
        out_specs=VMEM,
        compiler_params=params(),
        cost_estimate=pl.CostEstimate(flops=1_000_000_000, bytes_accessed=6 << 20, transcendentals=0),
        name="column_terms",
    )(block, rank, items)


def first_blocks_kernel(label, arrived, out):
    out[...] = jnp.zeros(out.shape, F32)
    parts, piece = out.shape[0], out.shape[2]

    def step(q, _):
        code = label[q] - 1

        @pl.when((code == 0) | (code == 4))
        def _():
            il = code // 4
            x, y = arrived[q, :N, :RANK], arrived[q, :N, RANK:]
            at = (slice(None), il)
            out[at] = out[at] + outer(x, y).reshape(parts, piece, N)

        return 0

    lax.fori_loop(0, arrived.shape[0], step, 0)


def first_blocks(label, arrived, ncol):
    return pl.pallas_call(
        first_blocks_kernel,
        out_shape=jax.ShapeDtypeStruct((ncol, 2, N // ncol, N), F32),
        in_specs=[SMEM, VMEM],
        out_specs=VMEM,
        compiler_params=params(),
        cost_estimate=pl.CostEstimate(flops=1_000_000_000, bytes_accessed=6 << 20, transcendentals=0),
        name="first_blocks",
    )(label, arrived)


def other_blocks_kernel(label, arrived, out, rows):
    out[...] = jnp.zeros(out.shape, F32)
    rows[...] = jnp.zeros(rows.shape, F32)
    parts, piece = rows.shape[0], rows.shape[2]

    def step(q, _):
        code = label[q] - 1
        il = code // 4
        jl = code - 4 * il

        @pl.when(code >= 0)
        def _():
            x = arrived[q, :N, :RANK]
            at = (slice(None), il)
            rows[at] = rows[at] + outer(x, x).reshape(parts, piece, N)

        @pl.when((code >= 0) & (jl > 0))
        def _():
            x, y = arrived[q, :N, :RANK], arrived[q, :N, RANK:]
            at = jnp.where(il == 0, 0, jl)
            out[at] = out[at] + outer(x, y)

        return 0

    lax.fori_loop(0, arrived.shape[0], step, 0)


def other_blocks(label, arrived, ncol):
    return pl.pallas_call(
        other_blocks_kernel,
        out_shape=(
            jax.ShapeDtypeStruct((4, N, N), F32),
            jax.ShapeDtypeStruct((ncol, 2, N // ncol, N), F32),
        ),
        in_specs=[SMEM, VMEM],
        out_specs=(VMEM,) * 2,
        compiler_params=params(),
        cost_estimate=pl.CostEstimate(flops=2_000_000_000, bytes_accessed=10 << 20, transcendentals=0),
        name="other_blocks",
    )(label, arrived)


def split(value):
    high = value.astype(BF16)
    return high, (value - high.astype(F32)).astype(BF16)


def trailing_kernel(place, first, other, panel, mirror, out):
    il, m = pl.program_id(0), pl.program_id(1)
    i = place[0] + place[2] * il
    j = place[1] + place[3] * m
    keep = (i > j) & (j >= 2)

    @pl.when(jnp.logical_not(keep))
    def _():
        out[...] = jnp.zeros(out.shape, F32)

    @pl.when(keep)
    def _():
        high, low = split(panel[0])
        other_side = mirror[0]
        update = outer(high, other_side) + outer(low, other_side)

        @pl.when(m == 0)
        def _():
            out[0, 0] = first[0] - update

        @pl.when(m > 0)
        def _():
            out[0, 0] = other[0] - update


def trailing_update(place, first, other, panel, mirror):
    brows, bcols = panel.shape[0], mirror.shape[0]
    return pl.pallas_call(
        trailing_kernel,
        grid=(brows, bcols),
        out_shape=jax.ShapeDtypeStruct((brows, bcols, N, N), F32),
        in_specs=[
            SMEM,
            pl.BlockSpec((1, N, N), lambda il, m: (il, 0, 0)),
            pl.BlockSpec((1, N, N), lambda il, m: (il * m, 0, 0)),
            pl.BlockSpec((1, N, 2 * N), lambda il, m: (il, 0, 0)),
            pl.BlockSpec((1, N, 2 * N), lambda il, m: (m, 0, 0)),
        ],
        out_specs=pl.BlockSpec((1, 1, N, N), lambda il, m: (il, m, 0, 0)),
        compiler_params=params(),
        cost_estimate=pl.CostEstimate(flops=8_000_000_000, bytes_accessed=20 << 20, transcendentals=0),
        name="trailing_update",
    )(place, first, other, panel, mirror)


def trailing_diagonal_kernel(place, diag, panel, out):
    i = place[0] + place[2] * pl.program_id(0)

    @pl.when(i < 2)
    def _():
        out[...] = jnp.zeros(out.shape, F32)

    @pl.when(i >= 2)
    def _():
        high, low = split(panel[0])
        out[0] = diag[0] - (outer(high, high) + (outer(high, low) + outer(low, high)))


def trailing_diagonal_update(place, diag, panel):
    brows = panel.shape[0]
    return pl.pallas_call(
        trailing_diagonal_kernel,
        grid=(brows,),
        out_shape=jax.ShapeDtypeStruct((brows, N, N), F32),
        in_specs=[
            SMEM,
            pl.BlockSpec((1, N, N), lambda il: (il, 0, 0)),
            pl.BlockSpec((1, N, 2 * N), lambda il: (il, 0, 0)),
        ],
        out_specs=pl.BlockSpec((1, N, N), lambda il: (il, 0, 0)),
        compiler_params=params(),
        cost_estimate=pl.CostEstimate(flops=4_000_000_000, bytes_accessed=8 << 20, transcendentals=0),
        name="trailing_diagonal",
    )(place, diag, panel)


def exchange(value, axis):
    return lax.all_to_all(value, axis, split_axis=0, concat_axis=0, tiled=True)


def sum_everywhere(term, nrow, ncol):
    rows = term.shape[0]
    pieces = exchange(term.reshape(ncol, rows // ncol, N), "col")
    mine = (pieces[0] + pieces[1]).reshape(nrow, -1, WIDTH)
    part = jnp.sum(exchange(mine, "row"), axis=0)
    whole = exchange(jnp.broadcast_to(part[None], mine.shape), "row").reshape(rows // ncol, N)
    return lax.all_gather(whole, "col", axis=0, tiled=True)


def on_device(diag_base, items, item_rank, item_owner, item_block):
    nrow = lax.axis_size("row")
    ncol = lax.axis_size("col")
    row_index = lax.axis_index("row")
    col_index = lax.axis_index("col")
    brows = diag_base.shape[0]
    piece = N // ncol
    diag_own = diag_base[:, 0]
    held = items[0, 0]
    rank = item_rank[0, 0]
    owner = item_owner[0, 0]
    block = item_block[0, 0].reshape(-1)
    place = jnp.stack([row_index, col_index, jnp.int32(nrow), jnp.int32(ncol)]).astype(jnp.int32)

    with jax.named_scope("pivot_sums"):
        term_zero, term_one = pivot_terms(owner, block, rank, place, held, diag_own[0])
        pivot_zero = sum_everywhere(term_zero, nrow, ncol)
        pivot_one = sum_everywhere(term_one, nrow, ncol)

    with jax.named_scope("items"):
        buffer = pack(owner, block, rank, held, nrow)
        arrived = exchange(buffer, "row").reshape(nrow * CAP, ROWS, WIDTH)
        label = arrived[:, N, 0].astype(jnp.int32)

    swap = [
        ((e + ncol * h) * ncol + c, (c + ncol * h) * ncol + e)
        for h in range(nrow // ncol)
        for e in range(ncol)
        for c in range(ncol)
    ]
    with jax.named_scope("diagonal_columns"):
        col_terms = column_terms(block, rank, held, ncol)
        col_sum = lax.psum_scatter(col_terms, "row", scatter_dimension=0, tiled=False)
        col_sum = lax.ppermute(col_sum, ("row", "col"), swap)

    with jax.named_scope("front"):
        first = first_blocks(label, arrived, ncol)
        first_pieces = exchange(first, "col")
        other, row_terms = other_blocks(label, arrived, ncol)

    with jax.named_scope("pivots"):
        lower_zero, inv_zero = first_pivot(pivot_zero)
        sub_panel, lower_one, inv_one = second_pivot(pivot_one, inv_zero)

    with jax.named_scope("panels"):
        global_rows = jnp.arange(brows) * nrow + row_index
        f_zero = first_pieces[0].reshape(brows * piece, N)
        f_one = first_pieces[1].reshape(brows * piece, N)
        p_zero = mul_t(f_zero, inv_zero)
        p_one = mul_t(f_one - mul_t(p_zero, sub_panel), inv_one)
        part = jnp.concatenate([p_zero, p_one], axis=1).reshape(brows, piece, 2 * N)
        after = jnp.stack([global_rows > 0, global_rows > 1], axis=1)
        after = jnp.repeat(after, N, axis=1)[:, None, :]
        part = jnp.where(after, part, jnp.zeros_like(part))
        panel = lax.all_gather(part, "col", axis=0, tiled=False)
        panel = panel.transpose(1, 0, 2, 3).reshape(brows, N, 2 * N)

    with jax.named_scope("mirror"):
        mine = lax.ppermute(part.astype(BF16), ("row", "col"), swap)
        mirror = lax.all_gather(mine, "row", axis=0, tiled=False)
        mirror = mirror.reshape(nrow // ncol, ncol, brows, piece, 2 * N)
        mirror = mirror.transpose(2, 0, 1, 3, 4).reshape(brows * nrow // ncol, N, 2 * N)

    with jax.named_scope("diagonal"):
        row_sum = jnp.sum(exchange(row_terms, "col"), axis=0)
        own = lax.dynamic_slice_in_dim(diag_own, col_index * piece, piece, axis=1)
        diag = lax.all_gather(col_sum + row_sum + own, "col", axis=0, tiled=False)
        diag = diag.transpose(1, 0, 2, 3).reshape(brows, N, N)

    with jax.named_scope("trailing"):
        first_own = first.transpose(1, 0, 2, 3).reshape(brows, N, N)
        trailing = trailing_update(place, first_own, other, panel, mirror)[:, None, :, None]
        trailing_diagonal = trailing_diagonal_update(place, diag, panel)[:, None]
    diag_factors = jnp.stack([lower_zero, lower_one])
    return (diag_factors, panel[:, None], trailing_diagonal, trailing)


def solution(mesh):
    placed = (
        P(None, "row", None, None),
        P("row", "col", None, None, None),
        P("row", "col", None),
        P("row", "col", None),
        P("row", "col", None, None),
    )
    return jax.shard_map(
        on_device,
        mesh=mesh,
        in_specs=placed,
        out_specs=(
            P(),
            P(None, "row", None, None),
            P(None, "row", None, None),
            P(None, "row", None, "col", None, None),
        ),
        check_vma=False,
    )
```

```python
import functools

import jax
import jax.numpy as jnp
from jax import lax
from jax.experimental import pallas as pl
from jax.experimental.pallas import tpu as pltpu
from jax.sharding import PartitionSpec as P

HI = lax.Precision.HIGHEST
N = 512
NB = 128
RANK = 64
WIDTH = 128
LABEL_ROWS = 16
ROWS = N + LABEL_ROWS
CAP = 2
EXTRA = 8
F32 = jnp.float32
BF16 = jnp.bfloat16
VMEM = pl.BlockSpec(memory_space=pltpu.VMEM)
SMEM = pl.BlockSpec(memory_space=pltpu.SMEM)


def dotT(a,b):
    return lax.dot_general(a,b,(((0,),(0,)),((),())),precision=HI,preferred_element_type=F32)
def dot(a,b):
    return lax.dot_general(a,b,(((1,),(0,)),((),())),precision=HI,preferred_element_type=F32)
def lane(x,k):
    return jnp.broadcast_to(x[:,k:k+1],(8,128))
def sub(x,k):
    return jnp.broadcast_to(x[k:k+1,:],(8,x.shape[1]))
def factor_block(d, eye):
    A=[d[8*q:8*q+8,:] for q in range(16)]
    Z=[eye[8*q:8*q+8,:] for q in range(16)]
    sl=lax.broadcasted_iota(jnp.int32,(8,128),0)
    for g in range(4):
        for p in range(4*g,4*g+4):
            S=[lane(A[p],8*p+k) for k in range(8)]
            T={q:[lane(A[q],8*p+k) for k in range(8)] for q in range(p+1,4*g+4)}
            a,z=A[p],Z[p]
            rows=[]
            for j in range(8):
                r=lax.rsqrt(sub(S[j],j))
                c=S[j]*r
                u=[sub(c,m) if m>j else None for m in range(8)]
                for m in range(j+1,8):
                    S[m]=S[m]-c*u[m]
                arow=sub(a,j)*r; zrow=sub(z,j)*r
                cm=jnp.where(sl>j,c,0.0)
                a=jnp.where(sl==j,arow,a-cm*arow)
                z=jnp.where(sl==j,zrow,z-cm*zrow)
                for q in T:
                    t=T[q][j]*r
                    for m in range(j+1,8):
                        T[q][m]=T[q][m]-t*u[m]
                    A[q]=A[q]-t*arow
                    Z[q]=Z[q]-t*zrow
            A[p],Z[p]=a,z
        if g<3:
            ug=jnp.concatenate(A[4*g:4*g+4],axis=0)
            zg=jnp.concatenate(Z[4*g:4*g+4],axis=0)
            both=jnp.concatenate([ug,zg],axis=1)
            upd=dotT(ug,both)
            for q in range(4*g+4,16):
                A[q]=A[q]-upd[8*q:8*q+8,:128]
                Z[q]=Z[q]-upd[8*q:8*q+8,128:]
    return jnp.concatenate(A,axis=0), jnp.concatenate(Z,axis=0)
def chol_into(work,l_ref,inv_ref):
    r128=lax.broadcasted_iota(jnp.int32,(NB,NB),0); c128=lax.broadcasted_iota(jnp.int32,(NB,NB),1)
    eye=jnp.where(r128==c128,1.0,0.0).astype(F32)
    nb=N//NB
    for b in range(nb):
        r0=b*NB; r1=r0+NB
        u,gi=factor_block(work[r0:r1,r0:r1],eye)
        u=jnp.where(c128>=r128,u,0.0); gi=jnp.where(c128<=r128,gi,0.0)
        l_ref[r0:r1,r0:r1]=u.T
        if b+1<nb: l_ref[r0:r1,r1:]=jnp.zeros((NB,N-r1),F32)
        inv_ref[r0:r1,r0:r1]=gi
        if b+1<nb: inv_ref[r0:r1,r1:]=jnp.zeros((NB,N-r1),F32)
        if b:
            inv_ref[r0:r1,:r0]=dot(gi,work[r0:r1,N:N+r0])
        if b+1<nb:
            ur=dot(gi,work[r0:r1,r1:N])
            l_ref[r1:,r0:r1]=ur.T
            work[r1:,r1:N]-=dotT(ur,ur)
            upd=dotT(ur,inv_ref[r0:r1,:r1])
            work[r1:,N:N+r1]-=upd

def params(mib=48):
    return pltpu.CompilerParams(vmem_limit_bytes=mib << 20)


def first_pivot_kernel(gathered, l_ref, inv_ref, work):
    rows = N // gathered.shape[0]
    for e in range(gathered.shape[0]):
        work[e * rows : (e + 1) * rows, :N] = gathered[e, :rows, :]
    work[:, N:] = jnp.zeros((N, N), F32)
    chol_into(work, l_ref, inv_ref)


def second_pivot_kernel(gathered, l0_ref, inv0_ref, p_ref, l_ref, inv_ref, work):
    l_ref[0] = l0_ref[...]
    count = gathered.shape[0]
    rows = N // count
    half = rows // 2
    top = [gathered[e, rows : rows + half, :] for e in range(count)]
    bottom = [gathered[e, 2 * rows + half :, :] for e in range(count)]
    p = mul_t(jnp.concatenate(top + bottom, axis=0), inv0_ref[...])
    p_ref[...] = p
    update = mul_t(p, p)
    for e in range(count):
        at = slice(e * rows, (e + 1) * rows)
        work[at, :N] = gathered[e, rows + half : 2 * rows + half, :] - update[at, :]
    work[:, N:] = jnp.zeros((N, N), F32)
    chol_into(work, l_ref.at[1], inv_ref)


def block_shape():
    return jax.ShapeDtypeStruct((N, N), F32)


def first_pivot(gathered):
    return pl.pallas_call(
        first_pivot_kernel,
        out_shape=(block_shape(),) * 2,
        in_specs=[VMEM],
        out_specs=(VMEM,) * 2,
        scratch_shapes=[pltpu.VMEM((N, 2 * N), F32)],
        compiler_params=params(),
        cost_estimate=pl.CostEstimate(flops=20_000_000_000, bytes_accessed=3 << 20, transcendentals=0),
        name="first_pivot",
    )(gathered)


def second_pivot(gathered, lower0, inv0):
    return pl.pallas_call(
        second_pivot_kernel,
        out_shape=(block_shape(), jax.ShapeDtypeStruct((2, N, N), F32), block_shape()),
        in_specs=[VMEM] * 3,
        out_specs=(VMEM,) * 3,
        scratch_shapes=[pltpu.VMEM((N, 2 * N), F32)],
        compiler_params=params(),
        cost_estimate=pl.CostEstimate(flops=20_000_000_000, bytes_accessed=6 << 20, transcendentals=0),
        name="second_pivot",
    )(gathered, lower0, inv0)


def mul_t(a, b):
    return lax.dot_general(a, b, (((1,), (1,)), ((), ())), precision=HI, preferred_element_type=F32)


def outer(a, b):
    return lax.dot_general(a, b, (((1,), (1,)), ((), ())), preferred_element_type=F32)


def keep_row(rank):
    lanes = lax.broadcasted_iota(jnp.int32, (1, WIDTH), 1)
    within = jnp.where(lanes >= RANK, lanes - RANK, lanes)
    return jnp.where(within < rank, 1.0, 0.0).astype(F32)


def pack_kernel(owner, block, rank, items, out, count):
    nrow = out.shape[0]

    def clear(o, _):
        count[o] = 0
        return 0

    lax.fori_loop(0, nrow, clear, 0)
    for slot in range(CAP):
        out[:, slot, N:, :] = jnp.zeros((nrow, LABEL_ROWS, WIDTH), BF16)

    def place(s, _):
        o = owner[s]
        slot = jnp.minimum(count[o], CAP - 1)
        count[o] = slot + 1
        keep = keep_row(rank[s])
        out[o, slot, :N, :] = items[s] * keep.astype(BF16)
        code = (block[2 * s] * 4 + block[2 * s + 1] + 1).astype(F32)
        out[o, slot, N:, :] = jnp.full((LABEL_ROWS, WIDTH), code, F32).astype(BF16)
        return 0

    lax.fori_loop(0, items.shape[0], place, 0)


def pack(owner, block, rank, items, nrow):
    return pl.pallas_call(
        pack_kernel,
        out_shape=jax.ShapeDtypeStruct((nrow, CAP, ROWS, WIDTH), BF16),
        in_specs=[SMEM, SMEM, SMEM, VMEM],
        out_specs=VMEM,
        scratch_shapes=[pltpu.SMEM((nrow,), jnp.int32)],
        compiler_params=params(),
        cost_estimate=pl.CostEstimate(flops=0, bytes_accessed=6 << 20, transcendentals=0),
        name="pack",
    )(owner, block, rank, items)


def pivot_terms_kernel(owner, block, rank, place, items, base, main, extra):
    row, col = place[0], place[1]
    main[...] = jnp.zeros((N, N), F32)
    extra[...] = jnp.zeros((2 * N, N), F32)

    @pl.when((row == 0) & (col == 0))
    def _():
        main[...] = base[...]

    @pl.when((row == 1) & (col == 0))
    def _():
        extra[N:, :] = base[...]

    def step(s, _):
        first = (block[2 * s + 1] == 0) & (col < 2)
        keep = keep_row(rank[s]).astype(BF16)

        @pl.when(first)
        def _():
            y = (items[s] * keep)[:, RANK:]
            main[...] += outer(y, y)

        @pl.when(first & (col == 0) & (owner[s] == 1) & (block[2 * s] == 0))
        def _():
            both = items[s] * keep
            x, y = both[:, :RANK], both[:, RANK:]
            extra[:N, :] += outer(x, y)
            extra[N:, :] += outer(x, x)

        return 0

    lax.fori_loop(0, items.shape[0], step, 0)


def pivot_terms(owner, block, rank, place, items, base):
    return pl.pallas_call(
        pivot_terms_kernel,
        out_shape=(block_shape(), jax.ShapeDtypeStruct((2 * N, N), F32)),
        in_specs=[SMEM] * 4 + [VMEM] * 2,
        out_specs=(VMEM,) * 2,
        compiler_params=params(),
        cost_estimate=pl.CostEstimate(flops=4_000_000_000, bytes_accessed=6 << 20, transcendentals=0),
        name="pivot_terms",
    )(owner, block, rank, place, items, base)


def pack_pair(lower, upper, out, base, piece):
    down = lax.broadcasted_iota(jnp.int32, (N, N), 0)
    across = lax.broadcasted_iota(jnp.int32, (N, N), 1)
    packed = jnp.where(down >= across, lower, upper)
    line = jnp.sum(jnp.where(down == across, upper, jnp.zeros_like(upper)), axis=0, keepdims=True)
    for e in range(N // piece):
        out[base + e, :piece, :] = packed[e * piece : (e + 1) * piece, :]
        out[base + e, piece:, :] = jnp.broadcast_to(line, (EXTRA, N))


def column_terms_kernel(block, rank, items, out, total):
    total[...] = jnp.zeros(total.shape, F32)
    heads = total.shape[0] // 2
    parts = out.shape[0] // heads

    def step(s, _):
        jl = block[2 * s + 1]
        y = (items[s] * keep_row(rank[s]).astype(BF16))[:, RANK:]
        total[jl] += outer(y, y)
        return 0

    lax.fori_loop(0, items.shape[0], step, 0)
    for h in range(heads):
        pack_pair(total[h], total[h + heads], out, h * parts, N // parts)


def column_terms(block, rank, items, ncol):
    return pl.pallas_call(
        column_terms_kernel,
        out_shape=jax.ShapeDtypeStruct((2 * ncol, N // ncol + EXTRA, N), F32),
        in_specs=[SMEM] * 2 + [VMEM],
        out_specs=VMEM,
        scratch_shapes=[pltpu.VMEM((4, N, N), F32)],
        compiler_params=params(),
        cost_estimate=pl.CostEstimate(flops=6_000_000_000, bytes_accessed=6 << 20, transcendentals=0),
        name="column_terms",
    )(block, rank, items)


def first_blocks_kernel(label, arrived, out):
    out[...] = jnp.zeros(out.shape, F32)
    parts, piece = out.shape[0], out.shape[2]

    def step(q, _):
        code = label[q] - 1

        @pl.when((code == 0) | (code == 4))
        def _():
            il = code // 4
            x, y = arrived[q, :N, :RANK], arrived[q, :N, RANK:]
            at = (slice(None), il)
            out[at] = out[at] + outer(x, y).reshape(parts, piece, N)

        return 0

    lax.fori_loop(0, arrived.shape[0], step, 0)


def first_blocks(label, arrived, ncol):
    return pl.pallas_call(
        first_blocks_kernel,
        out_shape=jax.ShapeDtypeStruct((ncol, 2, N // ncol, N), F32),
        in_specs=[SMEM, VMEM],
        out_specs=VMEM,
        compiler_params=params(),
        cost_estimate=pl.CostEstimate(flops=1_000_000_000, bytes_accessed=6 << 20, transcendentals=0),
        name="first_blocks",
    )(label, arrived)


def other_blocks_kernel(label, arrived, out, rows, total):
    out[...] = jnp.zeros(out.shape, F32)
    total[...] = jnp.zeros(total.shape, F32)

    def step(q, _):
        code = label[q] - 1
        il = code // 4
        jl = code - 4 * il

        @pl.when(code >= 0)
        def _():
            x = arrived[q, :N, :RANK]
            total[il] += outer(x, x)

        @pl.when((code >= 0) & (jl > 0))
        def _():
            x, y = arrived[q, :N, :RANK], arrived[q, :N, RANK:]
            at = jnp.where(il == 0, 0, jl)
            out[at] = out[at] + outer(x, y)

        return 0

    lax.fori_loop(0, arrived.shape[0], step, 0)
    pack_pair(total[0], total[1], rows, 0, N // rows.shape[0])


def other_blocks(label, arrived, ncol):
    return pl.pallas_call(
        other_blocks_kernel,
        out_shape=(
            jax.ShapeDtypeStruct((4, N, N), F32),
            jax.ShapeDtypeStruct((ncol, N // ncol + EXTRA, N), F32),
        ),
        in_specs=[SMEM, VMEM],
        out_specs=(VMEM,) * 2,
        scratch_shapes=[pltpu.VMEM((2, N, N), F32)],
        compiler_params=params(),
        cost_estimate=pl.CostEstimate(flops=8_000_000_000, bytes_accessed=10 << 20, transcendentals=0),
        name="other_blocks",
    )(label, arrived)


def split(value):
    high = value.astype(BF16)
    return high, (value - high.astype(F32)).astype(BF16)


def mul_t3(a, b):
    return outer(a[0], b[0]) + (outer(a[0], b[1]) + outer(a[1], b[0]))


def mul_t2(a, b):
    return outer(a, b[0]) + outer(a, b[1])


def by_lower(a, factor, product):
    half = N // 2
    top = tuple(ref[:half, :half] for ref in factor)
    bottom = tuple(ref[half:, :] for ref in factor)
    if isinstance(a, tuple):
        narrow = tuple(part[:, :half] for part in a)
    else:
        narrow = a[:, :half]
    return jnp.concatenate([product(narrow, top), product(a, bottom)], axis=1)


def rows_kernel(place, rows, base, inv0, sub, inv1, panel, high, diagonal, factors):
    brows = panel.shape[0]
    piece = N // rows.shape[0]
    for at, ref in enumerate((inv0, sub, inv1)):
        factors[2 * at], factors[2 * at + 1] = split(ref[...])
    pair = [(factors[2 * at], factors[2 * at + 1]) for at in range(3)]

    def gathered(at):
        return rows[:, at * piece : (at + 1) * piece, :].reshape(N, N)

    down = lax.broadcasted_iota(jnp.int32, (N, N), 0)
    across = lax.broadcasted_iota(jnp.int32, (N, N), 1)
    packed = gathered(2 * brows)
    line = rows[0, (2 * brows + 1) * piece : (2 * brows + 1) * piece + 1, :]
    none = jnp.zeros_like(packed)
    lower = jnp.where(down > across, packed, none)
    upper = jnp.where(down < across, packed, none)
    middle = (jnp.where(down == across, packed, none), jnp.where(down == across, line, none))
    for il, side in enumerate((lower, upper)):
        i = place[0] + place[2] * il
        left = by_lower(split(gathered(il)), pair[0], mul_t3)
        left = jnp.where(i > 0, left, none)
        right = gathered(brows + il) - mul_t3(split(left), pair[1])
        right = by_lower(split(right), pair[2], mul_t3)
        right = jnp.where(i > 1, right, none)
        panel[il, :, :N] = left
        panel[il, :, N:] = right
        a, b = split(panel[il])
        high[il] = a
        update = outer(a, a) + (outer(a, b) + outer(b, a))
        value = base[il] + (side + side.T + middle[il]) - update
        diagonal[il] = jnp.where(i > 1, value, none)


def solve_rows(place, rows, base, inv0, sub, inv1):
    brows = base.shape[0]
    return pl.pallas_call(
        rows_kernel,
        out_shape=(
            jax.ShapeDtypeStruct((brows, N, 2 * N), F32),
            jax.ShapeDtypeStruct((brows, N, 2 * N), BF16),
            jax.ShapeDtypeStruct((brows, N, N), F32),
            jax.ShapeDtypeStruct((6, N, N), BF16),
        ),
        in_specs=[SMEM] + [VMEM] * 5,
        out_specs=(VMEM,) * 4,
        compiler_params=params(),
        cost_estimate=pl.CostEstimate(flops=9_000_000_000, bytes_accessed=20 << 20, transcendentals=0),
        name="solve_rows",
    )(place, rows, base, inv0, sub, inv1)


def trailing_kernel(place, zero, one, factors, high, first, other, trailing):
    m = pl.program_id(0)
    pair = [(factors.at[2 * at], factors.at[2 * at + 1]) for at in range(3)]
    j = place[1] + place[3] * m
    left = by_lower(zero[0, :, 0, 0].reshape(N, N), pair[0], mul_t2).astype(BF16)
    middle = mul_t2(left, tuple(ref[...] for ref in pair[1]))
    right = one[0, :, 0, 0].reshape(N, N).astype(F32) - middle
    right = by_lower(right.astype(BF16), pair[2], mul_t2).astype(BF16)

    def update(il):
        return outer(high[il, :, :N], left) + outer(high[il, :, N:], right)

    for il in range(high.shape[0]):
        keep = (place[0] + place[2] * il > j) & (j >= 2)

        @pl.when(jnp.logical_not(keep))
        def _():
            trailing[il, 0] = jnp.zeros((N, N), F32)

        @pl.when(keep & (m == 0))
        def _():
            trailing[il, 0] = first[:, il].reshape(N, N) - update(il)

        @pl.when(keep & (m > 0))
        def _():
            trailing[il, 0] = other[il * m] - update(il)


def trailing_update(place, mirror, factors, high, first, other):
    ncol, brows, piece = first.shape[:3]
    heads = mirror.shape[0]
    bcols = heads * brows

    def mirrored(k):
        return pl.BlockSpec(
            (1, ncol, 1, 1, piece, N), lambda m: (lax.rem(m, heads), 0, k, lax.div(m, heads), 0, 0)
        )

    return pl.pallas_call(
        trailing_kernel,
        grid=(bcols,),
        out_shape=jax.ShapeDtypeStruct((brows, bcols, N, N), F32),
        in_specs=[SMEM, mirrored(0), mirrored(1)] + [VMEM] * 4,
        out_specs=pl.BlockSpec((brows, 1, N, N), lambda m: (0, m, 0, 0)),
        compiler_params=params(),
        cost_estimate=pl.CostEstimate(flops=9_000_000_000, bytes_accessed=20 << 20, transcendentals=0),
        name="trailing_update",
    )(place, mirror, mirror, factors, high, first, other)


def exchange(value, axis):
    return lax.all_to_all(value, axis, split_axis=0, concat_axis=0, tiled=True)


def after(value, *others):
    return lax.optimization_barrier((value,) + others)[0]


def on_device(diag_base, items, item_rank, item_owner, item_block):
    nrow = lax.axis_size("row")
    ncol = lax.axis_size("col")
    row_index = lax.axis_index("row")
    col_index = lax.axis_index("col")
    brows = diag_base.shape[0]
    piece = N // ncol
    half = piece // 2
    heads = nrow // ncol
    core = col_index % 2
    diag_own = diag_base[:, 0]
    held = items[0, 0]
    rank = item_rank[0, 0]
    owner = item_owner[0, 0]
    block = item_block[0, 0].reshape(-1)
    place = jnp.stack([row_index, col_index, jnp.int32(nrow), jnp.int32(ncol)]).astype(jnp.int32)
    partner = [(c, c ^ 1) for c in range(ncol)]

    swap, turn = [], []
    for h in range(heads):
        for e in range(ncol):
            for c in range(ncol):
                source = (c + ncol * h) * ncol + e
                swap.append((source, (e + ncol * h) * ncol + c))
                turn.append((source, ((e ^ 1) + ncol * h) * ncol + c))

    def from_first(pieces, axis=0):
        return [
            lax.ppermute(lax.index_in_dim(pieces, d, axis, False), "col", [(0, 2 * d), (1, 2 * d + 1)])
            for d in range(1, ncol // 2)
        ]

    with jax.named_scope("items"):
        buffer = pack(owner, block, rank, held, nrow)
        arrived = exchange(buffer, "row").reshape(nrow * CAP, ROWS, WIDTH)
        label = arrived[:, N, 0].astype(jnp.int32)

    with jax.named_scope("pivot_sums"):
        main, extra = pivot_terms(after(owner, buffer), block, rank, place, held, diag_own[0])
        handed = lax.ppermute(extra[N // 2 :], "col", [(0, 1)])
        whole_main = main + handed[N // 2 :]
        upper = jnp.where(col_index == 0, extra[: N // 2], handed[: N // 2])
        pieces = jnp.concatenate(
            [whole_main.reshape(ncol // 2, 2, piece, N), upper.reshape(ncol // 2, 2, half, N)], axis=2
        )
        got = functools.reduce(jnp.add, from_first(pieces), pieces[0])
        mine = lax.dynamic_index_in_dim(got, core, 0, False)
        given = lax.ppermute(lax.dynamic_index_in_dim(got, 1 - core, 0, False), "col", partner)
        mine = jnp.where(core == 0, jnp.concatenate([mine, given]), jnp.concatenate([given, mine]))
        spread = after(mine, arrived).reshape(nrow, -1, WIDTH)
        part = jnp.sum(exchange(spread, "row"), axis=0)

    with jax.named_scope("diagonal_columns"):
        col_terms = column_terms(after(block, main), rank, held, ncol)
        col_sum = lax.psum_scatter(col_terms, "row", scatter_dimension=0, tiled=False)
        col_sum = lax.ppermute(col_sum, ("row", "col"), swap)

    with jax.named_scope("front"):
        first = first_blocks(label, arrived, ncol)
        wide = first.reshape(ncol // 2, 2, brows, piece, N)
        got = functools.reduce(jnp.add, from_first(wide))
        got = jnp.where(col_index < 2, wide[0], got)
        kept = lax.dynamic_index_in_dim(got, core, 0, False)
        sent = lax.dynamic_index_in_dim(got, 1 - core, 0, False)
        straight = lax.ppermute(kept.astype(BF16), ("row", "col"), swap)
        turned = lax.ppermute(sent.astype(BF16), ("row", "col"), turn)
        even = row_index % 2 == 0
        both = jnp.where(even, jnp.stack([straight, turned]), jnp.stack([turned, straight]))
        given = lax.ppermute(sent, "col", partner)
        own_rows = jnp.where(core == 0, jnp.stack([kept, given]), jnp.stack([given, kept]))

    with jax.named_scope("pivot_spread"):
        spread = jnp.broadcast_to(after(part, first)[None], spread.shape)
        whole = exchange(spread, "row").reshape(-1, N)
        pivot = lax.all_gather(whole, "col", axis=0, tiled=False)

    with jax.named_scope("other_front"):
        other, row_terms = other_blocks(after(label, part), arrived, ncol)

    with jax.named_scope("diagonal"):
        row_sum = jnp.sum(exchange(after(row_terms, whole), "col"), axis=0)
        rows = jnp.concatenate([own_rows.reshape(2 * brows * piece, N), col_sum + row_sum])
        rows = lax.all_gather(rows, "col", axis=0, tiled=False)

    with jax.named_scope("mirror"):
        mirror = exchange(jnp.broadcast_to(after(both, row_sum)[None], (nrow,) + both.shape), "row")
        mirror = mirror.reshape(heads, ncol, 2, brows, piece, N)

    with jax.named_scope("pivots"):
        lower_zero, inv_zero = first_pivot(after(pivot, other))
        sub_panel, diag_factors, inv_one = second_pivot(pivot, lower_zero, inv_zero)

    with jax.named_scope("finish"):
        panel, high, diagonal, factors = solve_rows(
            place, rows, diag_own, inv_zero, sub_panel, inv_one
        )
        trailing = trailing_update(place, mirror, factors, high, first, other)
    return (diag_factors, panel[:, None], diagonal[:, None], trailing[:, None, :, None])


def solution(mesh):
    placed = (
        P(None, "row", None, None),
        P("row", "col", None, None, None),
        P("row", "col", None),
        P("row", "col", None),
        P("row", "col", None, None),
    )
    return jax.shard_map(
        on_device,
        mesh=mesh,
        in_specs=placed,
        out_specs=(
            P(),
            P(None, "row", None, None),
            P(None, "row", None, None),
            P(None, "row", None, "col", None, None),
        ),
        check_vma=False,
    )
```

```python
import functools

import jax
import jax.numpy as jnp
from jax import lax
from jax.experimental import pallas as pl
from jax.experimental.pallas import tpu as pltpu
from jax.sharding import PartitionSpec as P

HI = lax.Precision.HIGH
N = 512
NB = 128
RANK = 64
WIDTH = 128
LABEL_ROWS = 16
ROWS = N + LABEL_ROWS
CAP = 2
EXTRA = 8
F32 = jnp.float32
BF16 = jnp.bfloat16
VMEM = pl.BlockSpec(memory_space=pltpu.VMEM)
SMEM = pl.BlockSpec(memory_space=pltpu.SMEM)


def dotT(a,b):
    return lax.dot_general(a,b,(((0,),(0,)),((),())),precision=HI,preferred_element_type=F32)
def dot(a,b):
    return lax.dot_general(a,b,(((1,),(0,)),((),())),precision=HI,preferred_element_type=F32)
def lane(x,k):
    return jnp.broadcast_to(x[:,k:k+1],(8,128))
def sub(x,k):
    return jnp.broadcast_to(x[k:k+1,:],(8,x.shape[1]))
def factor_block(d, eye):
    A=[d[8*q:8*q+8,:] for q in range(16)]
    Z=[eye[8*q:8*q+8,:] for q in range(16)]
    sl=lax.broadcasted_iota(jnp.int32,(8,128),0)
    for g in range(4):
        for p in range(4*g,4*g+4):
            S=[lane(A[p],8*p+k) for k in range(8)]
            T={q:[lane(A[q],8*p+k) for k in range(8)] for q in range(p+1,4*g+4)}
            a,z=A[p],Z[p]
            rows=[]
            for j in range(8):
                r=lax.rsqrt(sub(S[j],j))
                c=S[j]*r
                u=[sub(c,m) if m>j else None for m in range(8)]
                for m in range(j+1,8):
                    S[m]=S[m]-c*u[m]
                arow=sub(a,j)*r; zrow=sub(z,j)*r
                cm=jnp.where(sl>j,c,0.0)
                a=jnp.where(sl==j,arow,a-cm*arow)
                z=jnp.where(sl==j,zrow,z-cm*zrow)
                for q in T:
                    t=T[q][j]*r
                    for m in range(j+1,8):
                        T[q][m]=T[q][m]-t*u[m]
                    A[q]=A[q]-t*arow
                    Z[q]=Z[q]-t*zrow
            A[p],Z[p]=a,z
        if g<3:
            ug=jnp.concatenate(A[4*g:4*g+4],axis=0)
            zg=jnp.concatenate(Z[4*g:4*g+4],axis=0)
            both=jnp.concatenate([ug,zg],axis=1)
            upd=dotT(ug,both)
            for q in range(4*g+4,16):
                A[q]=A[q]-upd[8*q:8*q+8,:128]
                Z[q]=Z[q]-upd[8*q:8*q+8,128:]
    return jnp.concatenate(A,axis=0), jnp.concatenate(Z,axis=0)
def chol_into(work,l_ref,inv_ref):
    r128=lax.broadcasted_iota(jnp.int32,(NB,NB),0); c128=lax.broadcasted_iota(jnp.int32,(NB,NB),1)
    eye=jnp.where(r128==c128,1.0,0.0).astype(F32)
    nb=N//NB
    for b in range(nb):
        r0=b*NB; r1=r0+NB
        u,gi=factor_block(work[r0:r1,r0:r1],eye)
        u=jnp.where(c128>=r128,u,0.0); gi=jnp.where(c128<=r128,gi,0.0)
        l_ref[r0:r1,r0:r1]=u.T
        if b+1<nb: l_ref[r0:r1,r1:]=jnp.zeros((NB,N-r1),F32)
        inv_ref[r0:r1,r0:r1]=gi
        if b+1<nb: inv_ref[r0:r1,r1:]=jnp.zeros((NB,N-r1),F32)
        if b:
            inv_ref[r0:r1,:r0]=dot(gi,work[r0:r1,N:N+r0])
        if b+1<nb:
            ur=dot(gi,work[r0:r1,r1:N])
            l_ref[r1:,r0:r1]=ur.T
            work[r1:,r1:N]-=dotT(ur,ur)
            upd=dotT(ur,inv_ref[r0:r1,:r1])
            work[r1:,N:N+r1]-=upd

def params(mib=48):
    return pltpu.CompilerParams(vmem_limit_bytes=mib << 20)


def first_pivot_kernel(gathered, l_ref, inv_ref, work):
    rows = N // gathered.shape[0]
    for e in range(gathered.shape[0]):
        work[e * rows : (e + 1) * rows, :N] = gathered[e, :rows, :]
    work[:, N:] = jnp.zeros((N, N), F32)
    chol_into(work, l_ref, inv_ref)


def second_pivot_kernel(gathered, l0_ref, inv0_ref, p_ref, l_ref, inv_ref, work):
    l_ref[0] = l0_ref[...]
    count = gathered.shape[0]
    rows = N // count
    half = rows // 2
    top = [gathered[e, rows : rows + half, :] for e in range(count)]
    bottom = [gathered[e, 2 * rows + half :, :] for e in range(count)]
    p = mul_t(jnp.concatenate(top + bottom, axis=0), inv0_ref[...])
    p_ref[...] = p
    update = mul_t(p, p)
    for e in range(count):
        at = slice(e * rows, (e + 1) * rows)
        work[at, :N] = gathered[e, rows + half : 2 * rows + half, :] - update[at, :]
    work[:, N:] = jnp.zeros((N, N), F32)
    chol_into(work, l_ref.at[1], inv_ref)


def block_shape():
    return jax.ShapeDtypeStruct((N, N), F32)


def first_pivot(gathered):
    return pl.pallas_call(
        first_pivot_kernel,
        out_shape=(block_shape(),) * 2,
        in_specs=[VMEM],
        out_specs=(VMEM,) * 2,
        scratch_shapes=[pltpu.VMEM((N, 2 * N), F32)],
        compiler_params=params(),
        cost_estimate=pl.CostEstimate(flops=20_000_000_000, bytes_accessed=3 << 20, transcendentals=0),
        name="first_pivot",
    )(gathered)


def second_pivot(gathered, lower0, inv0):
    return pl.pallas_call(
        second_pivot_kernel,
        out_shape=(block_shape(), jax.ShapeDtypeStruct((2, N, N), F32), block_shape()),
        in_specs=[VMEM] * 3,
        out_specs=(VMEM,) * 3,
        scratch_shapes=[pltpu.VMEM((N, 2 * N), F32)],
        compiler_params=params(),
        cost_estimate=pl.CostEstimate(flops=20_000_000_000, bytes_accessed=6 << 20, transcendentals=0),
        name="second_pivot",
    )(gathered, lower0, inv0)


def mul_t(a, b):
    return lax.dot_general(a, b, (((1,), (1,)), ((), ())), precision=HI, preferred_element_type=F32)


def outer(a, b):
    return lax.dot_general(a, b, (((1,), (1,)), ((), ())), preferred_element_type=F32)


def keep_row(rank):
    lanes = lax.broadcasted_iota(jnp.int32, (1, WIDTH), 1)
    within = jnp.where(lanes >= RANK, lanes - RANK, lanes)
    return jnp.where(within < rank, 1.0, 0.0).astype(F32)


def pack_kernel(owner, block, rank, items, out, count):
    nrow = out.shape[0]

    def clear(o, _):
        count[o] = 0
        return 0

    lax.fori_loop(0, nrow, clear, 0)
    for slot in range(CAP):
        out[:, slot, N:, :] = jnp.zeros((nrow, LABEL_ROWS, WIDTH), BF16)

    def place(s, _):
        o = owner[s]
        slot = jnp.minimum(count[o], CAP - 1)
        count[o] = slot + 1
        keep = keep_row(rank[s])
        out[o, slot, :N, :] = items[s] * keep.astype(BF16)
        code = (block[2 * s] * 4 + block[2 * s + 1] + 1).astype(F32)
        out[o, slot, N:, :] = jnp.full((LABEL_ROWS, WIDTH), code, F32).astype(BF16)
        return 0

    lax.fori_loop(0, items.shape[0], place, 0)


def pack(owner, block, rank, items, nrow):
    return pl.pallas_call(
        pack_kernel,
        out_shape=jax.ShapeDtypeStruct((nrow, CAP, ROWS, WIDTH), BF16),
        in_specs=[SMEM, SMEM, SMEM, VMEM],
        out_specs=VMEM,
        scratch_shapes=[pltpu.SMEM((nrow,), jnp.int32)],
        compiler_params=params(),
        cost_estimate=pl.CostEstimate(flops=0, bytes_accessed=6 << 20, transcendentals=0),
        name="pack",
    )(owner, block, rank, items)


def pivot_terms_kernel(owner, block, rank, place, items, base, main, extra):
    row, col = place[0], place[1]
    main[...] = jnp.zeros((N, N), F32)
    extra[...] = jnp.zeros((2 * N, N), F32)

    @pl.when((row == 0) & (col == 0))
    def _():
        main[...] = base[...]

    @pl.when((row == 1) & (col == 0))
    def _():
        extra[N:, :] = base[...]

    def step(s, _):
        first = (block[2 * s + 1] == 0) & (col < 2)
        keep = keep_row(rank[s]).astype(BF16)

        @pl.when(first)
        def _():
            y = (items[s] * keep)[:, RANK:]
            main[...] += outer(y, y)

        @pl.when(first & (col == 0) & (owner[s] == 1) & (block[2 * s] == 0))
        def _():
            both = items[s] * keep
            x, y = both[:, :RANK], both[:, RANK:]
            extra[:N, :] += outer(x, y)
            extra[N:, :] += outer(x, x)

        return 0

    lax.fori_loop(0, items.shape[0], step, 0)


def pivot_terms(owner, block, rank, place, items, base):
    return pl.pallas_call(
        pivot_terms_kernel,
        out_shape=(block_shape(), jax.ShapeDtypeStruct((2 * N, N), F32)),
        in_specs=[SMEM] * 4 + [VMEM] * 2,
        out_specs=(VMEM,) * 2,
        compiler_params=params(),
        cost_estimate=pl.CostEstimate(flops=4_000_000_000, bytes_accessed=6 << 20, transcendentals=0),
        name="pivot_terms",
    )(owner, block, rank, place, items, base)


def pack_pair(lower, upper, out, base, piece):
    down = lax.broadcasted_iota(jnp.int32, (N, N), 0)
    across = lax.broadcasted_iota(jnp.int32, (N, N), 1)
    packed = jnp.where(down >= across, lower, upper)
    line = jnp.sum(jnp.where(down == across, upper, jnp.zeros_like(upper)), axis=0, keepdims=True)
    for e in range(N // piece):
        out[base + e, :piece, :] = packed[e * piece : (e + 1) * piece, :]
        out[base + e, piece:, :] = jnp.broadcast_to(line, (EXTRA, N))


def column_terms_kernel(block, rank, items, out, total):
    total[...] = jnp.zeros(total.shape, F32)
    heads = total.shape[0] // 2
    parts = out.shape[0] // heads

    def step(s, _):
        jl = block[2 * s + 1]
        y = (items[s] * keep_row(rank[s]).astype(BF16))[:, RANK:]
        total[jl] += outer(y, y)
        return 0

    lax.fori_loop(0, items.shape[0], step, 0)
    for h in range(heads):
        pack_pair(total[h], total[h + heads], out, h * parts, N // parts)


def column_terms(block, rank, items, ncol):
    return pl.pallas_call(
        column_terms_kernel,
        out_shape=jax.ShapeDtypeStruct((2 * ncol, N // ncol + EXTRA, N), F32),
        in_specs=[SMEM] * 2 + [VMEM],
        out_specs=VMEM,
        scratch_shapes=[pltpu.VMEM((4, N, N), F32)],
        compiler_params=params(),
        cost_estimate=pl.CostEstimate(flops=6_000_000_000, bytes_accessed=6 << 20, transcendentals=0),
        name="column_terms",
    )(block, rank, items)


def first_blocks_kernel(label, arrived, out):
    out[...] = jnp.zeros(out.shape, F32)
    parts, piece = out.shape[0], out.shape[2]

    def step(q, _):
        code = label[q] - 1

        @pl.when((code == 0) | (code == 4))
        def _():
            il = code // 4
            x, y = arrived[q, :N, :RANK], arrived[q, :N, RANK:]
            at = (slice(None), il)
            out[at] = out[at] + outer(x, y).reshape(parts, piece, N)

        return 0

    lax.fori_loop(0, arrived.shape[0], step, 0)


def first_blocks(label, arrived, ncol):
    return pl.pallas_call(
        first_blocks_kernel,
        out_shape=jax.ShapeDtypeStruct((ncol, 2, N // ncol, N), F32),
        in_specs=[SMEM, VMEM],
        out_specs=VMEM,
        compiler_params=params(),
        cost_estimate=pl.CostEstimate(flops=1_000_000_000, bytes_accessed=6 << 20, transcendentals=0),
        name="first_blocks",
    )(label, arrived)


def other_blocks_kernel(label, arrived, out, rows, total):
    out[...] = jnp.zeros(out.shape, F32)
    total[...] = jnp.zeros(total.shape, F32)

    def step(q, _):
        code = label[q] - 1
        il = code // 4
        jl = code - 4 * il

        @pl.when(code >= 0)
        def _():
            x = arrived[q, :N, :RANK]
            total[il] += outer(x, x)

        @pl.when((code >= 0) & (jl > 0))
        def _():
            x, y = arrived[q, :N, :RANK], arrived[q, :N, RANK:]
            at = jnp.where(il == 0, 0, jl)
            out[at] = out[at] + outer(x, y)

        return 0

    lax.fori_loop(0, arrived.shape[0], step, 0)
    pack_pair(total[0], total[1], rows, 0, N // rows.shape[0])


def other_blocks(label, arrived, ncol):
    return pl.pallas_call(
        other_blocks_kernel,
        out_shape=(
            jax.ShapeDtypeStruct((4, N, N), F32),
            jax.ShapeDtypeStruct((ncol, N // ncol + EXTRA, N), F32),
        ),
        in_specs=[SMEM, VMEM],
        out_specs=(VMEM,) * 2,
        scratch_shapes=[pltpu.VMEM((2, N, N), F32)],
        compiler_params=params(),
        cost_estimate=pl.CostEstimate(flops=8_000_000_000, bytes_accessed=10 << 20, transcendentals=0),
        name="other_blocks",
    )(label, arrived)


def split(value):
    high = value.astype(BF16)
    return high, (value - high.astype(F32)).astype(BF16)


def mul_t3(a, b):
    return outer(a[0], b[0]) + (outer(a[0], b[1]) + outer(a[1], b[0]))


def mul_t2(a, b):
    return outer(a, b[0]) + outer(a, b[1])


def by_lower(a, factor, product):
    half = N // 2
    top = tuple(ref[:half, :half] for ref in factor)
    bottom = tuple(ref[half:, :] for ref in factor)
    if isinstance(a, tuple):
        narrow = tuple(part[:, :half] for part in a)
    else:
        narrow = a[:, :half]
    return jnp.concatenate([product(narrow, top), product(a, bottom)], axis=1)


def rows_kernel(place, rows, base, inv0, sub, inv1, panel, high, diagonal, factors):
    brows = panel.shape[0]
    piece = N // rows.shape[0]
    for at, ref in enumerate((inv0, sub, inv1)):
        factors[2 * at], factors[2 * at + 1] = split(ref[...])
    pair = [(factors[2 * at], factors[2 * at + 1]) for at in range(3)]

    def gathered(at):
        return rows[:, at * piece : (at + 1) * piece, :].reshape(N, N)

    down = lax.broadcasted_iota(jnp.int32, (N, N), 0)
    across = lax.broadcasted_iota(jnp.int32, (N, N), 1)
    packed = gathered(2 * brows)
    line = rows[0, (2 * brows + 1) * piece : (2 * brows + 1) * piece + 1, :]
    none = jnp.zeros_like(packed)
    lower = jnp.where(down > across, packed, none)
    upper = jnp.where(down < across, packed, none)
    middle = (jnp.where(down == across, packed, none), jnp.where(down == across, line, none))
    for il, side in enumerate((lower, upper)):
        i = place[0] + place[2] * il
        left = by_lower(split(gathered(il)), pair[0], mul_t3)
        left = jnp.where(i > 0, left, none)
        right = gathered(brows + il) - mul_t3(split(left), pair[1])
        right = by_lower(split(right), pair[2], mul_t3)
        right = jnp.where(i > 1, right, none)
        panel[il, :, :N] = left
        panel[il, :, N:] = right
        a, b = split(panel[il])
        high[il] = a
        update = outer(a, a) + (outer(a, b) + outer(b, a))
        value = base[il] + (side + side.T + middle[il]) - update
        diagonal[il] = jnp.where(i > 1, value, none)


def solve_rows(place, rows, base, inv0, sub, inv1):
    brows = base.shape[0]
    return pl.pallas_call(
        rows_kernel,
        out_shape=(
            jax.ShapeDtypeStruct((brows, N, 2 * N), F32),
            jax.ShapeDtypeStruct((brows, N, 2 * N), BF16),
            jax.ShapeDtypeStruct((brows, N, N), F32),
            jax.ShapeDtypeStruct((6, N, N), BF16),
        ),
        in_specs=[SMEM] + [VMEM] * 5,
        out_specs=(VMEM,) * 4,
        compiler_params=params(),
        cost_estimate=pl.CostEstimate(flops=9_000_000_000, bytes_accessed=20 << 20, transcendentals=0),
        name="solve_rows",
    )(place, rows, base, inv0, sub, inv1)


def trailing_kernel(place, zero, one, factors, high, first, other, trailing):
    m = pl.program_id(0)
    pair = [(factors.at[2 * at], factors.at[2 * at + 1]) for at in range(3)]
    j = place[1] + place[3] * m
    left = by_lower(zero[0, :, 0, 0].reshape(N, N), pair[0], mul_t2).astype(BF16)
    middle = mul_t2(left, tuple(ref[...] for ref in pair[1]))
    right = one[0, :, 0, 0].reshape(N, N).astype(F32) - middle
    right = by_lower(right.astype(BF16), pair[2], mul_t2).astype(BF16)

    def update(il):
        return outer(high[il, :, :N], left) + outer(high[il, :, N:], right)

    for il in range(high.shape[0]):
        keep = (place[0] + place[2] * il > j) & (j >= 2)

        @pl.when(jnp.logical_not(keep))
        def _():
            trailing[il, 0] = jnp.zeros((N, N), F32)

        @pl.when(keep & (m == 0))
        def _():
            trailing[il, 0] = first[:, il].reshape(N, N) - update(il)

        @pl.when(keep & (m > 0))
        def _():
            trailing[il, 0] = other[il * m] - update(il)


def trailing_update(place, mirror, factors, high, first, other):
    ncol, brows, piece = first.shape[:3]
    heads = mirror.shape[0]
    bcols = heads * brows

    def mirrored(k):
        return pl.BlockSpec(
            (1, ncol, 1, 1, piece, N), lambda m: (lax.rem(m, heads), 0, k, lax.div(m, heads), 0, 0)
        )

    return pl.pallas_call(
        trailing_kernel,
        grid=(bcols,),
        out_shape=jax.ShapeDtypeStruct((brows, bcols, N, N), F32),
        in_specs=[SMEM, mirrored(0), mirrored(1)] + [VMEM] * 4,
        out_specs=pl.BlockSpec((brows, 1, N, N), lambda m: (0, m, 0, 0)),
        compiler_params=params(),
        cost_estimate=pl.CostEstimate(flops=9_000_000_000, bytes_accessed=20 << 20, transcendentals=0),
        name="trailing_update",
    )(place, mirror, mirror, factors, high, first, other)


def exchange(value, axis):
    return lax.all_to_all(value, axis, split_axis=0, concat_axis=0, tiled=True)


def after(value, *others):
    return lax.optimization_barrier((value,) + others)[0]


def on_device(diag_base, items, item_rank, item_owner, item_block):
    nrow = lax.axis_size("row")
    ncol = lax.axis_size("col")
    row_index = lax.axis_index("row")
    col_index = lax.axis_index("col")
    brows = diag_base.shape[0]
    piece = N // ncol
    half = piece // 2
    heads = nrow // ncol
    core = col_index % 2
    diag_own = diag_base[:, 0]
    held = items[0, 0]
    rank = item_rank[0, 0]
    owner = item_owner[0, 0]
    block = item_block[0, 0].reshape(-1)
    place = jnp.stack([row_index, col_index, jnp.int32(nrow), jnp.int32(ncol)]).astype(jnp.int32)
    partner = [(c, c ^ 1) for c in range(ncol)]

    swap, turn = [], []
    for h in range(heads):
        for e in range(ncol):
            for c in range(ncol):
                source = (c + ncol * h) * ncol + e
                swap.append((source, (e + ncol * h) * ncol + c))
                turn.append((source, ((e ^ 1) + ncol * h) * ncol + c))

    def from_first(pieces, axis=0):
        return [
            lax.ppermute(lax.index_in_dim(pieces, d, axis, False), "col", [(0, 2 * d), (1, 2 * d + 1)])
            for d in range(1, ncol // 2)
        ]

    with jax.named_scope("items"):
        buffer = pack(owner, block, rank, held, nrow)
        arrived = exchange(buffer, "row").reshape(nrow * CAP, ROWS, WIDTH)
        label = arrived[:, N, 0].astype(jnp.int32)

    with jax.named_scope("pivot_sums"):
        main, extra = pivot_terms(after(owner, buffer), block, rank, place, held, diag_own[0])
        handed = lax.ppermute(extra[N // 2 :], "col", [(0, 1)])
        whole_main = main + handed[N // 2 :]
        upper = jnp.where(col_index == 0, extra[: N // 2], handed[: N // 2])
        pieces = jnp.concatenate(
            [whole_main.reshape(ncol // 2, 2, piece, N), upper.reshape(ncol // 2, 2, half, N)], axis=2
        )
        got = functools.reduce(jnp.add, from_first(pieces), pieces[0])
        mine = lax.dynamic_index_in_dim(got, core, 0, False)
        given = lax.ppermute(lax.dynamic_index_in_dim(got, 1 - core, 0, False), "col", partner)
        mine = jnp.where(core == 0, jnp.concatenate([mine, given]), jnp.concatenate([given, mine]))
        spread = after(mine, arrived).reshape(nrow, -1, WIDTH)
        part = jnp.sum(exchange(spread, "row"), axis=0)

    with jax.named_scope("diagonal_columns"):
        col_terms = column_terms(after(block, main), rank, held, ncol)
        col_sum = lax.psum_scatter(col_terms, "row", scatter_dimension=0, tiled=False)
        col_sum = lax.ppermute(col_sum, ("row", "col"), swap)

    with jax.named_scope("front"):
        first = first_blocks(label, arrived, ncol)
        wide = first.reshape(ncol // 2, 2, brows, piece, N)
        got = functools.reduce(jnp.add, from_first(wide))
        got = jnp.where(col_index < 2, wide[0], got)
        kept = lax.dynamic_index_in_dim(got, core, 0, False)
        sent = lax.dynamic_index_in_dim(got, 1 - core, 0, False)
        straight = lax.ppermute(kept.astype(BF16), ("row", "col"), swap)
        turned = lax.ppermute(sent.astype(BF16), ("row", "col"), turn)
        even = row_index % 2 == 0
        both = jnp.where(even, jnp.stack([straight, turned]), jnp.stack([turned, straight]))
        given = lax.ppermute(sent, "col", partner)
        own_rows = jnp.where(core == 0, jnp.stack([kept, given]), jnp.stack([given, kept]))

    with jax.named_scope("pivot_spread"):
        spread = jnp.broadcast_to(after(part, first)[None], spread.shape)
        whole = exchange(spread, "row").reshape(-1, N)
        pivot = lax.all_gather(whole, "col", axis=0, tiled=False)

    with jax.named_scope("other_front"):
        other, row_terms = other_blocks(after(label, part), arrived, ncol)

    with jax.named_scope("diagonal"):
        row_sum = jnp.sum(exchange(after(row_terms, whole), "col"), axis=0)
        rows = jnp.concatenate([own_rows.reshape(2 * brows * piece, N), col_sum + row_sum])
        rows = lax.all_gather(rows, "col", axis=0, tiled=False)

    with jax.named_scope("mirror"):
        mirror = exchange(jnp.broadcast_to(after(both, row_sum)[None], (nrow,) + both.shape), "row")
        mirror = mirror.reshape(heads, ncol, 2, brows, piece, N)

    with jax.named_scope("pivots"):
        lower_zero, inv_zero = first_pivot(after(pivot, other))
        sub_panel, diag_factors, inv_one = second_pivot(pivot, lower_zero, inv_zero)

    with jax.named_scope("finish"):
        panel, high, diagonal, factors = solve_rows(
            place, rows, diag_own, inv_zero, sub_panel, inv_one
        )
        trailing = trailing_update(place, mirror, factors, high, first, other)
    return (diag_factors, panel[:, None], diagonal[:, None], trailing[:, None, :, None])


def solution(mesh):
    placed = (
        P(None, "row", None, None),
        P("row", "col", None, None, None),
        P("row", "col", None),
        P("row", "col", None),
        P("row", "col", None, None),
    )
    return jax.shard_map(
        on_device,
        mesh=mesh,
        in_specs=placed,
        out_specs=(
            P(),
            P(None, "row", None, None),
            P(None, "row", None, None),
            P(None, "row", None, "col", None, None),
        ),
        check_vma=False,
    )
```

```python
import functools

import jax
import jax.numpy as jnp
from jax import lax
from jax.experimental import pallas as pl
from jax.experimental.pallas import tpu as pltpu
from jax.sharding import PartitionSpec as P

HI = lax.Precision.HIGH
N = 512
NB = 128
RANK = 64
WIDTH = 128
LABEL_ROWS = 16
ROWS = N + LABEL_ROWS
CAP = 2
EXTRA = 8
F32 = jnp.float32
BF16 = jnp.bfloat16
VMEM = pl.BlockSpec(memory_space=pltpu.VMEM)
SMEM = pl.BlockSpec(memory_space=pltpu.SMEM)


def dotT(a,b):
    return lax.dot_general(a,b,(((0,),(0,)),((),())),precision=HI,preferred_element_type=F32)
def dot(a,b):
    return lax.dot_general(a,b,(((1,),(0,)),((),())),precision=HI,preferred_element_type=F32)
def lane(x,k):
    return jnp.broadcast_to(x[:,k:k+1],(8,128))
def sub(x,k):
    return jnp.broadcast_to(x[k:k+1,:],(8,x.shape[1]))
def factor_block(d, eye):
    A=[d[8*q:8*q+8,:] for q in range(16)]
    Z=[eye[8*q:8*q+8,:] for q in range(16)]
    sl=lax.broadcasted_iota(jnp.int32,(8,128),0)
    for g in range(4):
        for p in range(4*g,4*g+4):
            S=[lane(A[p],8*p+k) for k in range(8)]
            T={q:[lane(A[q],8*p+k) for k in range(8)] for q in range(p+1,4*g+4)}
            a,z=A[p],Z[p]
            rows=[]
            for j in range(8):
                r=lax.rsqrt(sub(S[j],j))
                c=S[j]*r
                u=[sub(c,m) if m>j else None for m in range(8)]
                for m in range(j+1,8):
                    S[m]=S[m]-c*u[m]
                arow=sub(a,j)*r; zrow=sub(z,j)*r
                cm=jnp.where(sl>j,c,0.0)
                a=jnp.where(sl==j,arow,a-cm*arow)
                z=jnp.where(sl==j,zrow,z-cm*zrow)
                for q in T:
                    t=T[q][j]*r
                    for m in range(j+1,8):
                        T[q][m]=T[q][m]-t*u[m]
                    A[q]=A[q]-t*arow
                    Z[q]=Z[q]-t*zrow
            A[p],Z[p]=a,z
        if g<3:
            ug=jnp.concatenate(A[4*g:4*g+4],axis=0)
            zg=jnp.concatenate(Z[4*g:4*g+4],axis=0)
            both=jnp.concatenate([ug,zg],axis=1)
            upd=dotT(ug,both)
            for q in range(4*g+4,16):
                A[q]=A[q]-upd[8*q:8*q+8,:128]
                Z[q]=Z[q]-upd[8*q:8*q+8,128:]
    return jnp.concatenate(A,axis=0), jnp.concatenate(Z,axis=0)
def chol_into(work,l_ref,inv_ref):
    r128=lax.broadcasted_iota(jnp.int32,(NB,NB),0); c128=lax.broadcasted_iota(jnp.int32,(NB,NB),1)
    eye=jnp.where(r128==c128,1.0,0.0).astype(F32)
    nb=N//NB
    for b in range(nb):
        r0=b*NB; r1=r0+NB
        u,gi=factor_block(work[r0:r1,r0:r1],eye)
        u=jnp.where(c128>=r128,u,0.0); gi=jnp.where(c128<=r128,gi,0.0)
        l_ref[r0:r1,r0:r1]=u.T
        if b+1<nb: l_ref[r0:r1,r1:]=jnp.zeros((NB,N-r1),F32)
        inv_ref[r0:r1,r0:r1]=gi
        if b+1<nb: inv_ref[r0:r1,r1:]=jnp.zeros((NB,N-r1),F32)
        if b:
            inv_ref[r0:r1,:r0]=dot(gi,work[r0:r1,N:N+r0])
        if b+1<nb:
            ur=dot(gi,work[r0:r1,r1:N])
            l_ref[r1:,r0:r1]=ur.T
            work[r1:,r1:N]-=dotT(ur,ur)
            upd=dotT(ur,inv_ref[r0:r1,:r1])
            work[r1:,N:N+r1]-=upd

def params(mib=48):
    return pltpu.CompilerParams(vmem_limit_bytes=mib << 20)


def first_pivot_kernel(gathered, l_ref, inv_ref, work):
    rows = N // gathered.shape[0]
    for e in range(gathered.shape[0]):
        work[e * rows : (e + 1) * rows, :N] = gathered[e, :rows, :]
    work[:, N:] = jnp.zeros((N, N), F32)
    chol_into(work, l_ref, inv_ref)


def second_pivot_kernel(gathered, l0_ref, inv0_ref, p_ref, l_ref, inv_ref, work):
    l_ref[0] = l0_ref[...]
    count = gathered.shape[0]
    rows = N // count
    half = rows // 2
    top = [gathered[e, rows : rows + half, :] for e in range(count)]
    bottom = [gathered[e, 2 * rows + half :, :] for e in range(count)]
    p = mul_t(jnp.concatenate(top + bottom, axis=0), inv0_ref[...])
    p_ref[...] = p
    update = mul_t(p, p)
    for e in range(count):
        at = slice(e * rows, (e + 1) * rows)
        work[at, :N] = gathered[e, rows + half : 2 * rows + half, :] - update[at, :]
    work[:, N:] = jnp.zeros((N, N), F32)
    chol_into(work, l_ref.at[1], inv_ref)


def block_shape():
    return jax.ShapeDtypeStruct((N, N), F32)


def first_pivot(gathered):
    return pl.pallas_call(
        first_pivot_kernel,
        out_shape=(block_shape(),) * 2,
        in_specs=[VMEM],
        out_specs=(VMEM,) * 2,
        scratch_shapes=[pltpu.VMEM((N, 2 * N), F32)],
        compiler_params=params(),
        cost_estimate=pl.CostEstimate(flops=20_000_000_000, bytes_accessed=3 << 20, transcendentals=0),
        name="first_pivot",
    )(gathered)


def second_pivot(gathered, lower0, inv0):
    return pl.pallas_call(
        second_pivot_kernel,
        out_shape=(block_shape(), jax.ShapeDtypeStruct((2, N, N), F32), block_shape()),
        in_specs=[VMEM] * 3,
        out_specs=(VMEM,) * 3,
        scratch_shapes=[pltpu.VMEM((N, 2 * N), F32)],
        compiler_params=params(),
        cost_estimate=pl.CostEstimate(flops=20_000_000_000, bytes_accessed=6 << 20, transcendentals=0),
        name="second_pivot",
    )(gathered, lower0, inv0)


def mul_t(a, b):
    return lax.dot_general(a, b, (((1,), (1,)), ((), ())), precision=HI, preferred_element_type=F32)


def outer(a, b):
    return lax.dot_general(a, b, (((1,), (1,)), ((), ())), preferred_element_type=F32)


def keep_row(rank):
    lanes = lax.broadcasted_iota(jnp.int32, (1, WIDTH), 1)
    within = jnp.where(lanes >= RANK, lanes - RANK, lanes)
    return jnp.where(within < rank, 1.0, 0.0).astype(F32)


def pack_kernel(owner, block, rank, items, out, count):
    nrow = out.shape[0]

    def clear(o, _):
        count[o] = 0
        return 0

    lax.fori_loop(0, nrow, clear, 0)
    for slot in range(CAP):
        out[:, slot, N:, :] = jnp.zeros((nrow, LABEL_ROWS, WIDTH), BF16)

    def place(s, _):
        o = owner[s]
        slot = jnp.minimum(count[o], CAP - 1)
        count[o] = slot + 1
        keep = keep_row(rank[s])
        out[o, slot, :N, :] = items[s] * keep.astype(BF16)
        code = (block[2 * s] * 4 + block[2 * s + 1] + 1).astype(F32)
        out[o, slot, N:, :] = jnp.full((LABEL_ROWS, WIDTH), code, F32).astype(BF16)
        return 0

    lax.fori_loop(0, items.shape[0], place, 0)


def pack(owner, block, rank, items, nrow):
    return pl.pallas_call(
        pack_kernel,
        out_shape=jax.ShapeDtypeStruct((nrow, CAP, ROWS, WIDTH), BF16),
        in_specs=[SMEM, SMEM, SMEM, VMEM],
        out_specs=VMEM,
        scratch_shapes=[pltpu.SMEM((nrow,), jnp.int32)],
        compiler_params=params(),
        cost_estimate=pl.CostEstimate(flops=0, bytes_accessed=6 << 20, transcendentals=0),
        name="pack",
    )(owner, block, rank, items)


def pivot_terms_kernel(owner, block, rank, place, items, base, main, extra):
    row, col = place[0], place[1]
    main[...] = jnp.zeros((N, N), F32)
    extra[...] = jnp.zeros((2 * N, N), F32)

    @pl.when((row == 0) & (col == 0))
    def _():
        main[...] = base[...]

    @pl.when((row == 1) & (col == 0))
    def _():
        extra[N:, :] = base[...]

    def step(s, _):
        first = (block[2 * s + 1] == 0) & (col < 2)
        keep = keep_row(rank[s]).astype(BF16)

        @pl.when(first)
        def _():
            y = (items[s] * keep)[:, RANK:]
            main[...] += outer(y, y)

        @pl.when(first & (col == 0) & (owner[s] == 1) & (block[2 * s] == 0))
        def _():
            both = items[s] * keep
            x, y = both[:, :RANK], both[:, RANK:]
            extra[:N, :] += outer(x, y)
            extra[N:, :] += outer(x, x)

        return 0

    lax.fori_loop(0, items.shape[0], step, 0)


def pivot_terms(owner, block, rank, place, items, base):
    return pl.pallas_call(
        pivot_terms_kernel,
        out_shape=(block_shape(), jax.ShapeDtypeStruct((2 * N, N), F32)),
        in_specs=[SMEM] * 4 + [VMEM] * 2,
        out_specs=(VMEM,) * 2,
        compiler_params=params(),
        cost_estimate=pl.CostEstimate(flops=4_000_000_000, bytes_accessed=6 << 20, transcendentals=0),
        name="pivot_terms",
    )(owner, block, rank, place, items, base)


def pack_pair(lower, upper, out, base, piece):
    down = lax.broadcasted_iota(jnp.int32, (N, N), 0)
    across = lax.broadcasted_iota(jnp.int32, (N, N), 1)
    packed = jnp.where(down >= across, lower, upper)
    line = jnp.sum(jnp.where(down == across, upper, jnp.zeros_like(upper)), axis=0, keepdims=True)
    for e in range(N // piece):
        out[base + e, :piece, :] = packed[e * piece : (e + 1) * piece, :]
        out[base + e, piece:, :] = jnp.broadcast_to(line, (EXTRA, N))


def column_terms_kernel(block, rank, items, out, total):
    total[...] = jnp.zeros(total.shape, F32)
    heads = total.shape[0] // 2
    parts = out.shape[0] // heads

    def step(s, _):
        jl = block[2 * s + 1]
        y = (items[s] * keep_row(rank[s]).astype(BF16))[:, RANK:]
        total[jl] += outer(y, y)
        return 0

    lax.fori_loop(0, items.shape[0], step, 0)
    for h in range(heads):
        pack_pair(total[h], total[h + heads], out, h * parts, N // parts)


def column_terms(block, rank, items, ncol):
    return pl.pallas_call(
        column_terms_kernel,
        out_shape=jax.ShapeDtypeStruct((2 * ncol, N // ncol + EXTRA, N), F32),
        in_specs=[SMEM] * 2 + [VMEM],
        out_specs=VMEM,
        scratch_shapes=[pltpu.VMEM((4, N, N), F32)],
        compiler_params=params(),
        cost_estimate=pl.CostEstimate(flops=6_000_000_000, bytes_accessed=6 << 20, transcendentals=0),
        name="column_terms",
    )(block, rank, items)


def first_blocks_kernel(label, arrived, out):
    out[...] = jnp.zeros(out.shape, F32)
    parts, piece = out.shape[0], out.shape[2]

    def step(q, _):
        code = label[q] - 1

        @pl.when((code == 0) | (code == 4))
        def _():
            il = code // 4
            x, y = arrived[q, :N, :RANK], arrived[q, :N, RANK:]
            at = (slice(None), il)
            out[at] = out[at] + outer(x, y).reshape(parts, piece, N)

        return 0

    lax.fori_loop(0, arrived.shape[0], step, 0)


def first_blocks(label, arrived, ncol):
    return pl.pallas_call(
        first_blocks_kernel,
        out_shape=jax.ShapeDtypeStruct((ncol, 2, N // ncol, N), F32),
        in_specs=[SMEM, VMEM],
        out_specs=VMEM,
        compiler_params=params(),
        cost_estimate=pl.CostEstimate(flops=1_000_000_000, bytes_accessed=6 << 20, transcendentals=0),
        name="first_blocks",
    )(label, arrived)


def other_blocks_kernel(label, arrived, out, rows, total):
    out[...] = jnp.zeros(out.shape, F32)
    total[...] = jnp.zeros(total.shape, F32)

    def step(q, _):
        code = label[q] - 1
        il = code // 4
        jl = code - 4 * il

        @pl.when(code >= 0)
        def _():
            x = arrived[q, :N, :RANK]
            total[il] += outer(x, x)

        @pl.when((code >= 0) & (jl > 0))
        def _():
            x, y = arrived[q, :N, :RANK], arrived[q, :N, RANK:]
            at = jnp.where(il == 0, 0, jl)
            out[at] = out[at] + outer(x, y)

        return 0

    lax.fori_loop(0, arrived.shape[0], step, 0)
    pack_pair(total[0], total[1], rows, 0, N // rows.shape[0])


def other_blocks(label, arrived, ncol):
    return pl.pallas_call(
        other_blocks_kernel,
        out_shape=(
            jax.ShapeDtypeStruct((4, N, N), F32),
            jax.ShapeDtypeStruct((ncol, N // ncol + EXTRA, N), F32),
        ),
        in_specs=[SMEM, VMEM],
        out_specs=(VMEM,) * 2,
        scratch_shapes=[pltpu.VMEM((2, N, N), F32)],
        compiler_params=params(),
        cost_estimate=pl.CostEstimate(flops=8_000_000_000, bytes_accessed=10 << 20, transcendentals=0),
        name="other_blocks",
    )(label, arrived)


def split(value):
    high = value.astype(BF16)
    return high, (value - high.astype(F32)).astype(BF16)


def mul_t3(a, b):
    return outer(a[0], b[0]) + (outer(a[0], b[1]) + outer(a[1], b[0]))


def mul_t2(a, b):
    return outer(a, b[0]) + outer(a, b[1])


def by_lower(a, factor, product):
    half = N // 2
    top = tuple(ref[:half, :half] for ref in factor)
    bottom = tuple(ref[half:, :] for ref in factor)
    if isinstance(a, tuple):
        narrow = tuple(part[:, :half] for part in a)
    else:
        narrow = a[:, :half]
    return jnp.concatenate([product(narrow, top), product(a, bottom)], axis=1)


def rows_kernel(place, rows, base, inv0, sub, inv1, panel, high, diagonal, factors):
    brows = panel.shape[0]
    piece = N // rows.shape[0]
    for at, ref in enumerate((inv0, sub, inv1)):
        factors[2 * at], factors[2 * at + 1] = split(ref[...])
    pair = [(factors[2 * at], factors[2 * at + 1]) for at in range(3)]

    def gathered(at):
        return rows[:, at * piece : (at + 1) * piece, :].reshape(N, N)

    down = lax.broadcasted_iota(jnp.int32, (N, N), 0)
    across = lax.broadcasted_iota(jnp.int32, (N, N), 1)
    packed = gathered(2 * brows)
    line = rows[0, (2 * brows + 1) * piece : (2 * brows + 1) * piece + 1, :]
    none = jnp.zeros_like(packed)
    lower = jnp.where(down > across, packed, none)
    upper = jnp.where(down < across, packed, none)
    middle = (jnp.where(down == across, packed, none), jnp.where(down == across, line, none))
    for il, side in enumerate((lower, upper)):
        i = place[0] + place[2] * il
        left = by_lower(split(gathered(il)), pair[0], mul_t3)
        left = jnp.where(i > 0, left, none)
        right = gathered(brows + il) - mul_t3(split(left), pair[1])
        right = by_lower(split(right), pair[2], mul_t3)
        right = jnp.where(i > 1, right, none)
        panel[il, :, :N] = left
        panel[il, :, N:] = right
        a, b = split(panel[il])
        high[il] = a
        side = side - outer(a, b)
        value = base[il] + (side + side.T + middle[il]) - outer(a, a)
        diagonal[il] = jnp.where(i > 1, value, none)


def solve_rows(place, rows, base, inv0, sub, inv1):
    brows = base.shape[0]
    return pl.pallas_call(
        rows_kernel,
        out_shape=(
            jax.ShapeDtypeStruct((brows, N, 2 * N), F32),
            jax.ShapeDtypeStruct((brows, N, 2 * N), BF16),
            jax.ShapeDtypeStruct((brows, N, N), F32),
            jax.ShapeDtypeStruct((6, N, N), BF16),
        ),
        in_specs=[SMEM] + [VMEM] * 5,
        out_specs=(VMEM,) * 4,
        compiler_params=params(),
        cost_estimate=pl.CostEstimate(flops=9_000_000_000, bytes_accessed=20 << 20, transcendentals=0),
        name="solve_rows",
    )(place, rows, base, inv0, sub, inv1)


def trailing_kernel(place, zero, one, factors, high, first, upper, lower, trailing):
    m = pl.program_id(0)
    pair = [(factors.at[2 * at], factors.at[2 * at + 1]) for at in range(3)]
    j = place[1] + place[3] * m
    left = by_lower(zero[0, :, 0, 0].reshape(N, N), pair[0], mul_t2).astype(BF16)
    middle = mul_t2(left, tuple(ref[...] for ref in pair[1]))
    right = one[0, :, 0, 0].reshape(N, N).astype(F32) - middle
    right = by_lower(right.astype(BF16), pair[2], mul_t2).astype(BF16)

    def update(il):
        return outer(high[il, :, :N], left) + outer(high[il, :, N:], right)

    for il in range(high.shape[0]):
        keep = (place[0] + place[2] * il > j) & (j >= 2)

        @pl.when(jnp.logical_not(keep))
        def _():
            trailing[il, 0] = jnp.zeros((N, N), F32)

        @pl.when(keep & (m == 0))
        def _():
            trailing[il, 0] = first[:, il].reshape(N, N) - update(il)

        @pl.when(keep & (m > 0))
        def _():
            trailing[il, 0] = (lower if il else upper)[0] - update(il)


def trailing_update(place, mirror, factors, high, first, other):
    ncol, brows, piece = first.shape[:3]
    heads = mirror.shape[0]
    bcols = heads * brows

    def mirrored(k):
        return pl.BlockSpec(
            (1, ncol, 1, 1, piece, N), lambda m: (lax.rem(m, heads), 0, k, lax.div(m, heads), 0, 0)
        )

    return pl.pallas_call(
        trailing_kernel,
        grid=(bcols,),
        out_shape=jax.ShapeDtypeStruct((brows, bcols, N, N), F32),
        in_specs=[SMEM, mirrored(0), mirrored(1)]
        + [VMEM] * 3
        + [pl.BlockSpec((1, N, N), lambda m: (0, 0, 0)), pl.BlockSpec((1, N, N), lambda m: (m, 0, 0))],
        out_specs=pl.BlockSpec((brows, 1, N, N), lambda m: (0, m, 0, 0)),
        compiler_params=params(),
        cost_estimate=pl.CostEstimate(flops=9_000_000_000, bytes_accessed=20 << 20, transcendentals=0),
        name="trailing_update",
    )(place, mirror, mirror, factors, high, first, other, other)


def exchange(value, axis):
    return lax.all_to_all(value, axis, split_axis=0, concat_axis=0, tiled=True)


def after(value, *others):
    return lax.optimization_barrier((value,) + others)[0]


def on_device(diag_base, items, item_rank, item_owner, item_block):
    nrow = lax.axis_size("row")
    ncol = lax.axis_size("col")
    row_index = lax.axis_index("row")
    col_index = lax.axis_index("col")
    brows = diag_base.shape[0]
    piece = N // ncol
    half = piece // 2
    heads = nrow // ncol
    core = col_index % 2
    diag_own = diag_base[:, 0]
    held = items[0, 0]
    rank = item_rank[0, 0]
    owner = item_owner[0, 0]
    block = item_block[0, 0].reshape(-1)
    place = jnp.stack([row_index, col_index, jnp.int32(nrow), jnp.int32(ncol)]).astype(jnp.int32)
    partner = [(c, c ^ 1) for c in range(ncol)]

    swap, turn = [], []
    for h in range(heads):
        for e in range(ncol):
            for c in range(ncol):
                source = (c + ncol * h) * ncol + e
                swap.append((source, (e + ncol * h) * ncol + c))
                turn.append((source, ((e ^ 1) + ncol * h) * ncol + c))

    def from_first(pieces, axis=0):
        return [
            lax.ppermute(lax.index_in_dim(pieces, d, axis, False), "col", [(0, 2 * d), (1, 2 * d + 1)])
            for d in range(1, ncol // 2)
        ]

    with jax.named_scope("items"):
        buffer = pack(owner, block, rank, held, nrow)
        arrived = exchange(buffer, "row").reshape(nrow * CAP, ROWS, WIDTH)
        label = arrived[:, N, 0].astype(jnp.int32)

    with jax.named_scope("pivot_sums"):
        main, extra = pivot_terms(after(owner, buffer), block, rank, place, held, diag_own[0])
        handed = lax.ppermute(extra[N // 2 :], "col", [(0, 1)])
        whole_main = main + handed[N // 2 :]
        upper = jnp.where(col_index == 0, extra[: N // 2], handed[: N // 2])
        pieces = jnp.concatenate(
            [whole_main.reshape(ncol // 2, 2, piece, N), upper.reshape(ncol // 2, 2, half, N)], axis=2
        )
        got = functools.reduce(jnp.add, from_first(pieces), pieces[0])
        mine = lax.dynamic_index_in_dim(got, core, 0, False)
        given = lax.ppermute(lax.dynamic_index_in_dim(got, 1 - core, 0, False), "col", partner)
        mine = jnp.where(core == 0, jnp.concatenate([mine, given]), jnp.concatenate([given, mine]))
        spread = after(mine, arrived).reshape(nrow, -1, WIDTH)
        part = jnp.sum(exchange(spread, "row"), axis=0)

    with jax.named_scope("diagonal_columns"):
        col_terms = column_terms(after(block, main), rank, held, ncol)
        col_sum = lax.psum_scatter(col_terms, "row", scatter_dimension=0, tiled=False)
        col_sum = lax.ppermute(col_sum, ("row", "col"), swap)

    with jax.named_scope("front"):
        first = first_blocks(label, arrived, ncol)
        wide = first.reshape(ncol // 2, 2, brows, piece, N)
        got = functools.reduce(jnp.add, from_first(wide))
        got = jnp.where(col_index < 2, wide[0], got)
        kept = lax.dynamic_index_in_dim(got, core, 0, False)
        sent = lax.dynamic_index_in_dim(got, 1 - core, 0, False)
        straight = lax.ppermute(kept.astype(BF16), ("row", "col"), swap)
        turned = lax.ppermute(sent.astype(BF16), ("row", "col"), turn)
        even = row_index % 2 == 0
        both = jnp.where(even, jnp.stack([straight, turned]), jnp.stack([turned, straight]))
        given = lax.ppermute(sent, "col", partner)
        own_rows = jnp.where(core == 0, jnp.stack([kept, given]), jnp.stack([given, kept]))

    with jax.named_scope("pivot_spread"):
        spread = jnp.broadcast_to(after(part, first)[None], spread.shape)
        whole = exchange(spread, "row").reshape(-1, N)
        pivot = lax.all_gather(whole, "col", axis=0, tiled=False)

    with jax.named_scope("other_front"):
        other, row_terms = other_blocks(after(label, part), arrived, ncol)

    with jax.named_scope("diagonal"):
        row_sum = jnp.sum(exchange(after(row_terms, whole), "col"), axis=0)
        rows = jnp.concatenate([own_rows.reshape(2 * brows * piece, N), col_sum + row_sum])
        rows = lax.all_gather(rows, "col", axis=0, tiled=False)

    with jax.named_scope("mirror"):
        mirror = exchange(jnp.broadcast_to(after(both, row_sum)[None], (nrow,) + both.shape), "row")
        mirror = mirror.reshape(heads, ncol, 2, brows, piece, N)

    with jax.named_scope("pivots"):
        lower_zero, inv_zero = first_pivot(after(pivot, other))
        sub_panel, diag_factors, inv_one = second_pivot(pivot, lower_zero, inv_zero)

    with jax.named_scope("finish"):
        panel, high, diagonal, factors = solve_rows(
            place, rows, diag_own, inv_zero, sub_panel, inv_one
        )
        trailing = trailing_update(place, mirror, factors, high, first, other)
    return (diag_factors, panel[:, None], diagonal[:, None], trailing[:, None, :, None])


def solution(mesh):
    placed = (
        P(None, "row", None, None),
        P("row", "col", None, None, None),
        P("row", "col", None),
        P("row", "col", None),
        P("row", "col", None, None),
    )
    return jax.shard_map(
        on_device,
        mesh=mesh,
        in_specs=placed,
        out_specs=(
            P(),
            P(None, "row", None, None),
            P(None, "row", None, None),
            P(None, "row", None, "col", None, None),
        ),
        check_vma=False,
    )
```
